256 devices in a mesh: row: 8 (over x_lo, y), col: 32 (over z, x_hi, core).
Axes of the slice: x: 4 (x_hi: 2, x_lo: 2; x = x_hi * 2 + x_lo), y: 4, z: 8, core: 2. Of those that a mesh axis runs over, the one named last changes fastest.
Arguments:
- corners: bfloat16 [8, 32, 128, 128], P('row', 'col'), may hold values from -6 to 6
- edges: bfloat16 [8, 32, 128, 4608], P('row', 'col'), may hold values from -0.5 to 0.5
- projectors: bfloat16 [32, 4608, 128], P('col'), may hold values from -0.09375 to 0.09375
- cotangent: bfloat16 [8, 32, 128, 128], P('row', 'col'), may hold values from -6 to 6
Outputs:
- corner_grad: bfloat16 [8, 32, 128, 128], P('row', 'col')
- edge_grad: bfloat16 [8, 32, 128, 4608], P('row', 'col')
- projector_grad: float32 [32, 4608, 128], P('col', 'row')
The draws below stay inside these ranges and needn't reach their ends.
All inputs are finite; a program needn't handle non-finite values.
Results may differ from the reference program's by a relative error of at most 0.028.
Values may be sent and summed in bfloat16 or wider, within the bound.
No kernel may reach another device: no remote copies, remote signals or barrier semaphores. Data moves between devices by JAX's collectives and lax.ppermute only.
A program may use at most 128 MiB of HBM per device.

```python
import jax
import jax.numpy as jnp
from jax import lax

D = 6
CHI = 128
MOVES = 6
ROWS = 8
COLS = 32


def steps_of(key, shape, shards, least, largest):
    loudness, own = 1.0, jax.random.fold_in(key, 6)
    for dim, shards_of in shards:
        draws = jnp.exp(jax.random.uniform(jax.random.fold_in(own, dim), (shards_of,), jnp.float32, least / len(shards), largest / len(shards)))
        loudness = loudness * jnp.repeat(draws, shape[dim] // shards_of).reshape([-1 if axis == dim else 1 for axis in range(len(shape))])
    return loudness


def bell_draw(key, dims, spread, most, shards=(), kind=jnp.bfloat16):
    level = steps_of(key, dims, shards, -0.22, 0.18) if shards else 1.0
    array = jax.random.normal(key, dims, jnp.float32) * spread * level
    return jnp.minimum(jnp.maximum(array, -most), most).astype(kind)


def setup_inputs(seed: int = 0) -> dict:
    arg_keys = jax.random.split(jax.random.key(seed), 5)
    corners = bell_draw(arg_keys[0], (ROWS, COLS, CHI, CHI), 1.0, 6.0, ((0, 8), (1, 32)))
    edges = bell_draw(arg_keys[1], (ROWS, COLS, CHI, D * D * CHI), CHI ** -0.5, 0.5, ((0, 8), (1, 32)))
    projectors = bell_draw(arg_keys[2], (COLS, CHI * D * D, CHI), (CHI * D * D) ** -0.5, 0.09375, ((0, 32),))
    cotangent = bell_draw(arg_keys[3], (ROWS, COLS, CHI, CHI), 1.0, 6.0, ((0, 8), (1, 32)))
    return dict(corners=corners, edges=edges, projectors=projectors, cotangent=cotangent)


def reference(corners, edges, projectors, cotangent):
    columns = corners.shape[1]
    chi_width = corners.shape[2]
    edge_width = edges.shape[3]
    projector_float = projectors.astype(jnp.float32)

    def row_pass(running, inputs):
        corner_row, edge_row, cot_row = inputs
        edge_float = edge_row.astype(jnp.float32)

        def merge_of(corner_now):
            product = jnp.einsum("lab,lbk->lak", corner_now.astype(jnp.float32), edge_float)
            return product.astype(jnp.bfloat16).reshape(columns, edge_width, chi_width)

        states = []
        corner_now = corner_row
        for move_index in range(MOVES):
            states.append(corner_now)
            if move_index + 1 < MOVES:
                merged = merge_of(corner_now)
                absorbed = jnp.einsum("lpi,lpb->lib", projector_float, merged.astype(jnp.float32)).astype(jnp.bfloat16)
                corner_now = jnp.roll(absorbed, 1, axis=0)
        adjoint = cot_row
        proj_total = jnp.zeros((columns, edge_width, chi_width), jnp.float32)
        edge_total = jnp.zeros((columns, chi_width, edge_width), jnp.float32)
        for move_index in reversed(range(MOVES)):
            arrived = jnp.roll(adjoint, -1, axis=0).astype(jnp.float32)
            merged = merge_of(states[move_index])
            merged_bar = jnp.einsum("lpi,lib->lpb", projector_float, arrived).astype(jnp.bfloat16)
            proj_total = proj_total + jnp.einsum("lpb,lib->lpi", merged.astype(jnp.float32), arrived)
            flat_bar = merged_bar.reshape(columns, chi_width, edge_width).astype(jnp.float32)
            edge_total = edge_total + jnp.einsum("lab,lak->lbk", states[move_index].astype(jnp.float32), flat_bar)
            adjoint = jnp.einsum("lak,lbk->lab", flat_bar, edge_float).astype(jnp.bfloat16)
        return running + proj_total, (adjoint, edge_total.astype(jnp.bfloat16))

    start_sum = jnp.zeros((columns, edge_width, chi_width), jnp.float32)
    proj_sum, (corner_grad, edge_grad) = lax.scan(row_pass, start_sum, (corners, edges, cotangent))
    return corner_grad, edge_grad, proj_sum
```

```python
import jax
import jax.numpy as jnp
from jax import lax
from jax.experimental import pallas as pl
from jax.experimental.pallas import tpu as pltpu
from jax.sharding import PartitionSpec as P


W = 128
BF = jnp.bfloat16
F32 = jnp.float32


def dot(a, b):
    return jnp.dot(a, b, preferred_element_type=F32)


def step(z, x_ref, y_ref):
    n = z.shape[0] // W
    total = None
    for t in range(x_ref.shape[1] // (2 * W)):
        cols = slice(2 * W * t, 2 * W * (t + 1))
        mid = dot(z, x_ref[:, cols]).astype(BF)
        tall = jnp.concatenate(
            [jnp.concatenate([mid[W * b : W * (b + 1), :W], mid[W * b : W * (b + 1), W:]], 0) for b in range(n)], 1
        )
        part = dot(y_ref[:, cols], tall)
        total = part if total is None else total + part
    return total.astype(BF)


def split(wide):
    return [wide[:, W * b : W * (b + 1)] for b in range(wide.shape[1] // W)]


def by_role(core_ref, body, edge, turned):
    @pl.when(core_ref[0] == 0)
    def _():
        body(edge, turned)

    @pl.when(core_ref[0] != 0)
    def _():
        body(turned, edge)


def turn_kernel(proj_ref, cot_ref, turned_ref, cot_t_ref, wide_ref):
    planes = turned_ref.shape[1] // W
    wide_ref[...] = proj_ref[...].astype(F32)
    for p in range(planes):
        turned_ref[:, W * p : W * (p + 1)] = wide_ref[pl.ds(p, W, stride=planes), :].T.astype(BF)
    cot_t_ref[...] = cot_ref[...].astype(F32).T.astype(BF)


def own_kernel(corner_ref, edge_ref, turned_ref, cot_t_ref, out_ref):
    out_ref[:W, :] = step(corner_ref[...], edge_ref, turned_ref)
    out_ref[W:, :] = cot_t_ref[...]


def first_kernel(core_ref, own_ref, mate_ref, edge_ref, turned_ref, out_ref):
    def body(x_ref, y_ref):
        start = jnp.where(core_ref[0] == 0, own_ref[:W, :], own_ref[W:, :])
        out_ref[:W, :] = jnp.where(core_ref[0] == 0, mate_ref[:W, :], mate_ref[W:, :])
        out_ref[W:, :] = step(start, x_ref, y_ref)

    by_role(core_ref, body, edge_ref, turned_ref)


def double_kernel(core_ref, come_ref, edge_ref, turned_ref, mate_edge_ref, mate_turned_ref, near_ref, far_ref):
    def run(x1, y1, x2, y2):
        near = jnp.concatenate(split(step(come_ref[...], x1, y1)), 0)
        near_ref[...] = near
        far_ref[...] = jnp.concatenate(split(step(near, x2, y2)), 0)

    @pl.when(core_ref[0] == 0)
    def _():
        run(edge_ref, turned_ref, mate_edge_ref, mate_turned_ref)

    @pl.when(core_ref[0] != 0)
    def _():
        run(turned_ref, edge_ref, mate_turned_ref, mate_edge_ref)


def last_kernel(core_ref, come_ref, edge_ref, turned_ref, mate_edge_ref, mate_turned_ref, out_ref, own_ref):
    @pl.when(core_ref[0] != 0)
    def _():
        got = split(step(come_ref[...], turned_ref, edge_ref))
        out_ref[:W, :] = got[0]
        own_ref[...] = got[1]
        out_ref[W:, :] = step(got[0], mate_turned_ref, mate_edge_ref)

    @pl.when(core_ref[0] == 0)
    def _():
        out_ref[...] = jnp.zeros_like(out_ref)
        own_ref[...] = jnp.zeros_like(own_ref)


def blocks(ref):
    return [ref[W * b : W * (b + 1), :] for b in range(ref.shape[0] // W)]


def fill(ref, parts):
    for b, part in enumerate(parts):
        ref[W * b : W * (b + 1), :] = part


def pairs_of(z_ref, x_ref, w_ref, put):
    n = z_ref.shape[0] // W
    for t in range(x_ref.shape[1] // (2 * W)):
        mid = dot(z_ref[...], x_ref[:, 2 * W * t : 2 * W * (t + 1)]).astype(BF)
        for half in range(2):
            flat = jnp.concatenate([mid[W * k : W * (k + 1), W * half : W * (half + 1)] for k in range(n)], 1)
            put(2 * t + half, dot(flat, w_ref[...]))


def proj_early_kernel(core_ref, r1_ref, r2_ref, m2_ref, m3_ref, edge_ref, out_ref, z_ref, w_ref):
    r1, r2, m2, m3 = blocks(r1_ref), blocks(r2_ref), blocks(m2_ref), blocks(m3_ref)

    @pl.when(core_ref[0] == 0)
    def _():
        fill(z_ref, [r1[0], r1[1], r2[0], r2[1]])
        fill(w_ref, [m3[1], m3[0], m2[1], m2[0]])

    @pl.when(core_ref[0] != 0)
    def _():
        fill(z_ref, [m2[0], m2[1], m3[0], m3[1]])
        fill(w_ref, [r2[1], r2[0], r1[1], r1[0]])

    def put(p, value):
        out_ref[:, W * p : W * (p + 1)] = value

    pairs_of(z_ref, edge_ref, w_ref, put)


def proj_late_kernel(core_ref, corner_ref, r3_ref, m1_ref, m4_ref, edge_ref, early_ref, out_ref, z_ref, w_ref):
    r3, m1, m4 = blocks(r3_ref), blocks(m1_ref), blocks(m4_ref)

    @pl.when(core_ref[0] == 0)
    def _():
        fill(z_ref, [corner_ref[...], r3[0]])
        fill(w_ref, [m4[0], m1[1]])

    @pl.when(core_ref[0] != 0)
    def _():
        fill(z_ref, [corner_ref[...], m1[0]])
        fill(w_ref, [r3[1], r3[0]])

    def put(p, value):
        out_ref[:, W * p : W * (p + 1)] = (early_ref[:, W * p : W * (p + 1)] + value).astype(BF)

    pairs_of(z_ref, edge_ref, w_ref, put)


def edge_kernel(
    core_ref, corner_ref, r1_ref, r2_ref, r3_ref, m1_ref, m2_ref, m3_ref, m4_ref, own_ref, turned_ref,
    out_ref, grad_ref, z_ref, w_ref,
):
    r1, r2, r3 = blocks(r1_ref), blocks(r2_ref), blocks(r3_ref)
    m1, m2, m3, m4 = blocks(m1_ref), blocks(m2_ref), blocks(m3_ref), blocks(m4_ref)

    @pl.when(core_ref[0] == 0)
    def _():
        fill(w_ref, [corner_ref[...], r1[0], r1[1], r2[0], r2[1], r3[0]])
        fill(z_ref, [m4[0], m3[1], m3[0], m2[1], m2[0], m1[1]])
        grad_ref[...] = m4[1].astype(F32).T.astype(BF)

    @pl.when(core_ref[0] != 0)
    def _():
        fill(w_ref, [corner_ref[...], m1[0], m2[0], m2[1], m3[0], m3[1]])
        fill(z_ref, [r3[1], r3[0], r2[1], r2[0], r1[1], r1[0]])
        grad_ref[...] = own_ref[...].astype(F32).T.astype(BF)

    def put(p, value):
        out_ref[:, W * p : W * (p + 1)] = value.T.astype(BF)

    pairs_of(z_ref, turned_ref, w_ref, put)


def gather_kernel(parts_ref, out_ref):
    rows = parts_ref.shape[1]
    planes = parts_ref.shape[2] // W
    for p in range(planes):
        out_ref[pl.ds(p, rows, stride=planes), :] = jnp.sum(
            parts_ref[:, :, W * p : W * (p + 1)].astype(F32), axis=0
        )


def call(kernel, shapes, *args, scratch=(), flops=0):
    specs = [
        pl.BlockSpec(memory_space=pltpu.SMEM if arg.dtype == jnp.int32 else pltpu.VMEM) for arg in args
    ]
    moved = sum(arg.size * arg.dtype.itemsize for arg in args)
    single = len(shapes) == 1
    outs = [jax.ShapeDtypeStruct(shape, kind) for shape, kind in shapes]
    out_specs = [pl.BlockSpec(memory_space=pltpu.VMEM) for _ in shapes]
    return pl.pallas_call(
        kernel,
        out_shape=outs[0] if single else outs,
        in_specs=specs,
        out_specs=out_specs[0] if single else out_specs,
        scratch_shapes=[pltpu.VMEM(shape, kind) for shape, kind in scratch],
        compiler_params=pltpu.CompilerParams(vmem_limit_bytes=24 * 1024 * 1024),
        cost_estimate=pl.CostEstimate(flops=flops, bytes_accessed=moved, transcendentals=0),
    )(*args)


def shards(corners, edges, projectors, cotangent):
    corner = corners[0, 0]
    edge = edges[0, 0]
    projector = projectors[0]
    cot = cotangent[0, 0]
    width = edge.shape[1]
    rows = lax.axis_size("row")
    cols = lax.axis_size("col")
    core = (lax.axis_index("col") % 2).astype(jnp.int32).reshape(1)
    unit = 2 * W * W * width

    def swap(value):
        return lax.ppermute(value, "col", [(i, i ^ 1) for i in range(cols)])

    def onward(value):
        return lax.ppermute(value, "col", [(i, (i + (2 if i % 2 == 0 else -2)) % cols) for i in range(cols)])

    two = ((2 * W, W), BF)
    mate_edge = swap(edge)
    turned, cot_t = call(
        turn_kernel, [((W, width), BF), ((W, W), BF)], projector, cot, scratch=[((width, W), F32)], flops=unit
    )
    mate_turned = swap(turned)
    own = call(own_kernel, [two], corner, edge, turned, cot_t, flops=2 * unit)
    m1 = swap(own)
    go1 = call(first_kernel, [two], core, own, m1, mate_edge, mate_turned, flops=2 * unit)
    tensors = (edge, turned, mate_edge, mate_turned)
    r1 = onward(go1)
    s1, go2 = call(double_kernel, [two, two], core, r1, *tensors, flops=8 * unit)
    r2 = onward(go2)
    m2 = swap(s1)
    s2, go3 = call(double_kernel, [two, two], core, r2, *tensors, flops=8 * unit)
    r3 = onward(go3)
    m3 = swap(s2)
    early = call(
        proj_early_kernel, [((W, width), F32)], core, r1, r2, m2, m3, edge,
        scratch=[((4 * W, W), BF), ((4 * W, W), BF)], flops=8 * unit,
    )
    s3, own_grad = call(last_kernel, [two, ((W, W), BF)], core, r3, *tensors, flops=6 * unit)
    m4 = swap(s3)
    late = call(
        proj_late_kernel, [((W, width), BF)], core, corner, r3, m1, m4, edge, early,
        scratch=[((2 * W, W), BF), ((2 * W, W), BF)], flops=4 * unit,
    )
    share = W // rows
    parts = lax.all_to_all(late.reshape(rows, share, width), "row", 0, 0, tiled=True)
    edge_grad, corner_grad = call(
        edge_kernel, [((W, width), BF), ((W, W), BF)], core, corner, r1, r2, r3, m1, m2, m3, m4, own_grad, turned,
        scratch=[((6 * W, W), BF), ((6 * W, W), BF)], flops=12 * unit,
    )
    proj = call(gather_kernel, [((share * width // W, W), F32)], parts, flops=unit)
    return (corner_grad[None, None], edge_grad[None, None], proj[None])


def solution(mesh):
    placed = (
        P("row", "col", None, None),
        P("row", "col", None, None),
        P("col", None, None),
        P("row", "col", None, None),
    )
    return jax.shard_map(
        shards,
        mesh=mesh,
        in_specs=placed,
        out_specs=(P("row", "col", None, None), P("row", "col", None, None), P("col", "row", None)),
        check_vma=False,
    )
```

```python
import jax
import jax.numpy as jnp
from jax import lax
from jax.experimental import pallas as pl
from jax.experimental.pallas import tpu as pltpu
from jax.sharding import PartitionSpec as P


W = 128
BF = jnp.bfloat16
F32 = jnp.float32


def dot(a, b):
    return jnp.dot(a, b, preferred_element_type=F32)


def step(z, x_ref, y_ref):
    n = z.shape[0] // W
    total = None
    for t in range(x_ref.shape[1] // (2 * W)):
        cols = slice(2 * W * t, 2 * W * (t + 1))
        mid = dot(z, x_ref[:, cols]).astype(BF)
        tall = jnp.concatenate(
            [jnp.concatenate([mid[W * b : W * (b + 1), :W], mid[W * b : W * (b + 1), W:]], 0) for b in range(n)], 1
        )
        part = dot(y_ref[:, cols], tall)
        total = part if total is None else total + part
    return total.astype(BF)


def split(wide):
    return [wide[:, W * b : W * (b + 1)] for b in range(wide.shape[1] // W)]


def turn_kernel(proj_ref, cot_ref, turned_ref, cot_t_ref, wide_ref):
    planes = turned_ref.shape[1] // W
    wide_ref[...] = proj_ref[...].astype(F32)
    for p in range(planes):
        turned_ref[:, W * p : W * (p + 1)] = wide_ref[pl.ds(p, W, stride=planes), :].T.astype(BF)
    cot_t_ref[...] = cot_ref[...].astype(F32).T.astype(BF)


def own_kernel(core_ref, corner_ref, edge_ref, turned_ref, cot_t_ref, keep_ref, send_ref):
    moved = step(corner_ref[...], edge_ref, turned_ref)
    keep_ref[...] = jnp.where(core_ref[0] == 0, moved, cot_t_ref[...])
    send_ref[...] = jnp.where(core_ref[0] == 0, cot_t_ref[...], moved)


def by_role(core_ref, body, tensors):
    edge, turned, mate_edge, mate_turned = tensors

    @pl.when(core_ref[0] == 0)
    def _():
        body(edge, turned, mate_edge, mate_turned)

    @pl.when(core_ref[0] != 0)
    def _():
        body(turned, edge, mate_turned, mate_edge)


def ahead_kernel(core_ref, keep_ref, mate_edge_ref, mate_turned_ref, out_ref):
    def body(x1, y1, x2, y2):
        out_ref[...] = step(keep_ref[...], x2, y2)

    by_role(core_ref, body, (None, None, mate_edge_ref, mate_turned_ref))


def single_kernel(core_ref, come_ref, ahead_ref, e_ref, t_ref, me_ref, mt_ref, near_ref, far_ref):
    far_ref[:W, :] = ahead_ref[...]

    def body(x1, y1, x2, y2):
        near = step(come_ref[...], x1, y1)
        near_ref[...] = near
        far_ref[W:, :] = step(near, x2, y2)

    by_role(core_ref, body, (e_ref, t_ref, me_ref, mt_ref))


def double_kernel(core_ref, come_ref, e_ref, t_ref, me_ref, mt_ref, m1_ref, m2_ref, near_ref, far_ref):
    def body(x1, y1, x2, y2):
        near = jnp.concatenate(split(step(come_ref[...], x1, y1)), 0)
        near_ref[...] = near
        far_ref[...] = jnp.concatenate(split(step(near, x2, y2)), 0)

    by_role(core_ref, body, (e_ref, t_ref, me_ref, mt_ref))


def turn_back_kernel(core_ref, come_ref, e_ref, t_ref, early_ref, near_ref):
    @pl.when(core_ref[0] == 0)
    def _():
        near_ref[:W, :] = step(come_ref[:W, :], e_ref, t_ref)
        near_ref[W:, :] = jnp.zeros((W, W), BF)

    @pl.when(core_ref[0] != 0)
    def _():
        fill(near_ref, split(step(come_ref[...], t_ref, e_ref)))


def blocks(ref):
    return [ref[W * b : W * (b + 1), :] for b in range(ref.shape[0] // W)]


def fill(ref, parts):
    for b, part in enumerate(parts):
        ref[W * b : W * (b + 1), :] = part


def pairs_of(z_ref, x_ref, w_ref, put):
    n = z_ref.shape[0] // W
    for t in range(x_ref.shape[1] // (2 * W)):
        mid = dot(z_ref[...], x_ref[:, 2 * W * t : 2 * W * (t + 1)]).astype(BF)
        for half in range(2):
            flat = jnp.concatenate([mid[W * k : W * (k + 1), W * half : W * (half + 1)] for k in range(n)], 1)
            put(2 * t + half, dot(flat, w_ref[...]))


def proj_first_kernel(core_ref, r1_ref, m3_ref, edge_ref, out_ref, z_ref, w_ref):
    r1, m3 = blocks(r1_ref), blocks(m3_ref)

    @pl.when(core_ref[0] == 0)
    def _():
        fill(z_ref, r1)
        fill(w_ref, m3[::-1])

    @pl.when(core_ref[0] != 0)
    def _():
        fill(z_ref, m3)
        fill(w_ref, r1[::-1])

    def put(p, value):
        out_ref[:, W * p : W * (p + 1)] = value

    pairs_of(z_ref, edge_ref, w_ref, put)


def adder(from_ref, to_ref):
    def put(p, value):
        at = slice(W * p, W * (p + 1))
        to_ref[:, at] = (from_ref[:, at] + value).astype(to_ref.dtype)

    return put


def proj_second_kernel(
    core_ref, r2_ref, m1_ref, m2_ref, near_ref, edge_ref, me_ref, mt_ref, early_ref, far_ref, out_ref, z_ref, w_ref
):
    @pl.when(core_ref[0] == 0)
    def _():
        fill(z_ref, blocks(r2_ref))
        fill(w_ref, [m2_ref[...], m1_ref[...]])
        pairs_of(z_ref, edge_ref, w_ref, adder(early_ref, out_ref))
        far_ref[...] = jnp.zeros_like(far_ref)

    @pl.when(core_ref[0] != 0)
    def _():
        far_ref[...] = step(near_ref[:W, :], mt_ref, me_ref)


def proj_third_kernel(
    core_ref, corner_ref, r0_ref, r2_ref, m1_ref, m2_ref, m4_ref, edge_ref, early_ref, sum_ref, out_ref, z_ref, w_ref
):
    @pl.when(core_ref[0] == 0)
    def _():
        fill(z_ref, [corner_ref[...], r0_ref[...]])
        fill(w_ref, blocks(m4_ref)[::-1])
        two = slice(0, 2 * W)
        pairs_of(z_ref.at[two], edge_ref, w_ref.at[two], adder(early_ref, out_ref))

    @pl.when(core_ref[0] != 0)
    def _():
        fill(z_ref, [m1_ref[...], m2_ref[...], m4_ref[:W, :]])
        fill(w_ref, blocks(r2_ref)[::-1] + [r0_ref[...]])
        pairs_of(z_ref, edge_ref, w_ref, adder(early_ref, sum_ref))


def proj_last_kernel(core_ref, corner_ref, r3_ref, edge_ref, sum_ref, done_ref, out_ref):
    @pl.when(core_ref[0] != 0)
    def _():
        pairs_of(corner_ref, edge_ref, r3_ref, adder(sum_ref, out_ref))


def edge_kernel(
    core_ref, corner_ref, r0_ref, r1_ref, r2_ref, r3_ref, m1_ref, m2_ref, m3_ref, m4_ref, edge_ref, turned_ref,
    out_ref, grad_ref, z_ref, w_ref,
):
    come = [r0_ref[...]] + blocks(r1_ref) + blocks(r2_ref)
    mate = [m1_ref[...], m2_ref[...]] + blocks(m3_ref) + blocks(m4_ref)

    @pl.when(core_ref[0] == 0)
    def _():
        fill(w_ref, [corner_ref[...]] + come)
        fill(z_ref, mate[::-1])

    @pl.when(core_ref[0] != 0)
    def _():
        fill(w_ref, [corner_ref[...]] + mate[:5])
        fill(z_ref, [r3_ref[...]] + come[::-1])

    def put(p, value):
        out_ref[:, W * p : W * (p + 1)] = value.T.astype(BF)

    pairs_of(z_ref, turned_ref, w_ref, put)
    grad_ref[...] = step(z_ref[:W, :], turned_ref, edge_ref).astype(F32).T.astype(BF)


def gather_kernel(parts_ref, out_ref):
    rows = parts_ref.shape[1]
    planes = parts_ref.shape[2] // W
    for p in range(planes):
        out_ref[pl.ds(p, rows, stride=planes), :] = jnp.sum(
            parts_ref[:, :, W * p : W * (p + 1)].astype(F32), axis=0
        )


def call(kernel, shapes, *args, scratch=(), flops=0, order=(), alias=None):
    def space(n, arg):
        if n in order:
            return pl.ANY
        return pltpu.SMEM if arg.dtype == jnp.int32 else pltpu.VMEM

    moved = sum(arg.size * arg.dtype.itemsize for n, arg in enumerate(args) if n not in order)
    single = len(shapes) == 1
    outs = [jax.ShapeDtypeStruct(shape, kind) for shape, kind in shapes]
    out_specs = [pl.BlockSpec(memory_space=pltpu.VMEM) for _ in shapes]
    return pl.pallas_call(
        kernel,
        out_shape=outs[0] if single else outs,
        in_specs=[pl.BlockSpec(memory_space=space(n, arg)) for n, arg in enumerate(args)],
        out_specs=out_specs[0] if single else out_specs,
        scratch_shapes=[pltpu.VMEM(shape, kind) for shape, kind in scratch],
        input_output_aliases=alias or {},
        compiler_params=pltpu.CompilerParams(vmem_limit_bytes=16 * 1024 * 1024),
        cost_estimate=pl.CostEstimate(flops=flops, bytes_accessed=moved, transcendentals=0),
    )(*args)


def shards(corners, edges, projectors, cotangent):
    corner = corners[0, 0]
    edge = edges[0, 0]
    projector = projectors[0]
    cot = cotangent[0, 0]
    width = edge.shape[1]
    rows = lax.axis_size("row")
    cols = lax.axis_size("col")
    core = (lax.axis_index("col") % 2).astype(jnp.int32).reshape(1)
    unit = 2 * W * W * width

    def send(value, to):
        pairs = [(i, to(i) % cols) for i in range(cols) if to(i) is not None]
        return lax.ppermute(value, "col", pairs)

    def swap(value):
        return send(value, lambda i: i ^ 1)

    def onward(value):
        return send(value, lambda i: i + 2 if i % 2 == 0 else i - 2)

    one, two = ((W, W), BF), ((2 * W, W), BF)
    whole, wide = ((W, width), BF), ((W, width), F32)

    def stacks(n):
        return [((n * W, W), BF), ((n * W, W), BF)]

    mate_edge = swap(edge)
    turned, cot_t = call(turn_kernel, [whole, one], projector, cot, scratch=[((width, W), F32)], flops=unit)
    mate_turned = swap(turned)
    keep, first = call(own_kernel, [one, one], core, corner, edge, turned, cot_t, flops=2 * unit)
    r0 = send(first, lambda i: i - 1 if i % 2 == 0 else i + 1)
    tensors = (edge, turned, mate_edge, mate_turned)
    ahead = call(ahead_kernel, [one], core, keep, mate_edge, mate_turned, flops=2 * unit)
    near1, go1 = call(single_kernel, [one, two], core, r0, ahead, *tensors, flops=4 * unit)
    r1 = onward(go1)
    m1, m2 = swap(keep), swap(near1)
    near2, go2 = call(double_kernel, [two, two], core, r1, *tensors, m1, m2, flops=8 * unit, order=(6, 7))
    r2 = onward(go2)
    m3 = swap(near2)
    early = call(proj_first_kernel, [wide], core, r1, m3, edge, scratch=stacks(2), flops=4 * unit)
    near3 = call(turn_back_kernel, [two], core, r2, edge, turned, early, flops=4 * unit, order=(4,))
    m4 = swap(near3)
    go3, early = call(
        proj_second_kernel, [one, wide], core, r2, m1, m2, near3, edge, mate_edge, mate_turned, early,
        scratch=stacks(2), flops=4 * unit, alias={8: 1},
    )
    r3 = send(go3, lambda i: None if i % 2 == 0 else i - 2)
    part, done = call(
        proj_third_kernel, [wide, whole], core, corner, r0, r2, m1, m2, m4, edge, early,
        scratch=stacks(3), flops=6 * unit, alias={8: 0},
    )
    done = call(proj_last_kernel, [whole], core, corner, r3, edge, part, done, flops=2 * unit, alias={5: 0})
    share = W // rows
    parts = lax.all_to_all(done.reshape(rows, share, width), "row", 0, 0, tiled=True)
    edge_grad, corner_grad = call(
        edge_kernel, [whole, one], core, corner, r0, r1, r2, r3, m1, m2, m3, m4, edge, turned,
        scratch=stacks(6), flops=14 * unit,
    )
    proj = call(gather_kernel, [((share * width // W, W), F32)], parts, flops=unit)
    return (corner_grad[None, None], edge_grad[None, None], proj[None])


def solution(mesh):
    placed = (
        P("row", "col", None, None),
        P("row", "col", None, None),
        P("col", None, None),
        P("row", "col", None, None),
    )
    return jax.shard_map(
        shards,
        mesh=mesh,
        in_specs=placed,
        out_specs=(P("row", "col", None, None), P("row", "col", None, None), P("col", "row", None)),
        check_vma=False,
    )
```

```python
import jax
import jax.numpy as jnp
from jax import lax
from jax.experimental import pallas as pl
from jax.experimental.pallas import tpu as pltpu
from jax.sharding import PartitionSpec as P


W = 128
BF = jnp.bfloat16
F32 = jnp.float32


def dot(a, b):
    return jnp.dot(a, b, preferred_element_type=F32)


def step(z, x_ref, y_ref):
    n = z.shape[0] // W
    total = None
    for t in range(x_ref.shape[1] // (2 * W)):
        cols = slice(2 * W * t, 2 * W * (t + 1))
        mid = dot(z, x_ref[:, cols]).astype(BF)
        tall = jnp.concatenate(
            [jnp.concatenate([mid[W * b : W * (b + 1), :W], mid[W * b : W * (b + 1), W:]], 0) for b in range(n)], 1
        )
        part = dot(y_ref[:, cols], tall)
        total = part if total is None else total + part
    return total.astype(BF)


def split(wide):
    return [wide[:, W * b : W * (b + 1)] for b in range(wide.shape[1] // W)]


def start_kernel(
    core_ref, proj_ref, edge_ref, corner_ref, cot_ref, turned_ref, keep_ref, send_ref,
    proj_in, wide_ref, edge_in, corner_in, cot_in, proj_sem, sem,
):
    pieces = proj_sem.shape[0]
    size = proj_ref.shape[0] // pieces
    loads = []
    for n in range(pieces):
        at = pl.ds(n * size, size)
        loads.append(pltpu.make_async_copy(proj_ref.at[at], proj_in.at[at], proj_sem.at[n]))
    others = [
        pltpu.make_async_copy(cot_ref, cot_in, sem.at[0]),
        pltpu.make_async_copy(corner_ref, corner_in, sem.at[1]),
        pltpu.make_async_copy(edge_ref, edge_in, sem.at[2]),
    ]
    for copy in loads + others:
        copy.start()
    for n, copy in enumerate(loads):
        copy.wait()
        at = slice(n * size, (n + 1) * size)
        wide_ref[at, :] = proj_in[at, :].astype(F32)
    planes = turned_ref.shape[1] // W
    for p in range(planes):
        turned_ref[:, W * p : W * (p + 1)] = wide_ref[pl.ds(p, W, stride=planes), :].T.astype(BF)
    for copy in others:
        copy.wait()
    cot_t = cot_in[...].astype(F32).T.astype(BF)
    moved = step(corner_in[...], edge_in, turned_ref)
    keep_ref[...] = jnp.where(core_ref[0] == 0, moved, cot_t)
    send_ref[...] = jnp.where(core_ref[0] == 0, cot_t, moved)


def by_role(core_ref, body, tensors):
    edge, turned, mate_edge, mate_turned = tensors

    @pl.when(core_ref[0] == 0)
    def _():
        body(edge, turned, mate_edge, mate_turned)

    @pl.when(core_ref[0] != 0)
    def _():
        body(turned, edge, mate_turned, mate_edge)


def ahead_kernel(core_ref, keep_ref, far_edge_ref, far_turned_ref, out_ref, mate_edge_ref, mate_turned_ref, sem):
    copies = [
        pltpu.make_async_copy(far_edge_ref, mate_edge_ref, sem.at[0]),
        pltpu.make_async_copy(far_turned_ref, mate_turned_ref, sem.at[1]),
    ]
    for copy in copies:
        copy.start()
    for copy in copies:
        copy.wait()

    def body(x1, y1, x2, y2):
        out_ref[...] = step(keep_ref[...], x2, y2)

    by_role(core_ref, body, (None, None, mate_edge_ref, mate_turned_ref))


def single_kernel(core_ref, come_ref, ahead_ref, e_ref, t_ref, me_ref, mt_ref, near_ref, far_ref):
    far_ref[:W, :] = ahead_ref[...]

    def body(x1, y1, x2, y2):
        near = step(come_ref[...], x1, y1)
        near_ref[...] = near
        far_ref[W:, :] = step(near, x2, y2)

    by_role(core_ref, body, (e_ref, t_ref, me_ref, mt_ref))


def double_kernel(core_ref, come_ref, e_ref, t_ref, me_ref, mt_ref, m1_ref, m2_ref, near_ref, far_ref):
    def body(x1, y1, x2, y2):
        near = jnp.concatenate(split(step(come_ref[...], x1, y1)), 0)
        near_ref[...] = near
        far_ref[...] = jnp.concatenate(split(step(near, x2, y2)), 0)

    by_role(core_ref, body, (e_ref, t_ref, me_ref, mt_ref))


def turn_back_kernel(core_ref, come_ref, e_ref, t_ref, me_ref, mt_ref, early_ref, near_ref, far_ref):
    @pl.when(core_ref[0] == 0)
    def _():
        near_ref[...] = step(come_ref[:W, :], e_ref, t_ref)
        far_ref[...] = jnp.zeros_like(far_ref)

    @pl.when(core_ref[0] != 0)
    def _():
        near = step(come_ref[:W, :], t_ref, e_ref)
        near_ref[...] = near
        far_ref[...] = step(near, mt_ref, me_ref)


def blocks(ref):
    return [ref[W * b : W * (b + 1), :] for b in range(ref.shape[0] // W)]


def fill(ref, parts):
    for b, part in enumerate(parts):
        ref[W * b : W * (b + 1), :] = part


def pairs_of(z_ref, x_ref, w_ref, put):
    n = z_ref.shape[0] // W
    for t in range(x_ref.shape[1] // (2 * W)):
        mid = dot(z_ref[...], x_ref[:, 2 * W * t : 2 * W * (t + 1)]).astype(BF)
        for half in range(2):
            flat = jnp.concatenate([mid[W * k : W * (k + 1), W * half : W * (half + 1)] for k in range(n)], 1)
            put(2 * t + half, dot(flat, w_ref[...]))


def proj_first_kernel(core_ref, r1_ref, m3_ref, edge_ref, out_ref, z_ref, w_ref):
    r1, m3 = blocks(r1_ref), blocks(m3_ref)

    @pl.when(core_ref[0] == 0)
    def _():
        fill(z_ref, r1)
        fill(w_ref, m3[::-1])

    @pl.when(core_ref[0] != 0)
    def _():
        fill(z_ref, m3)
        fill(w_ref, r1[::-1])

    def put(p, value):
        out_ref[:, W * p : W * (p + 1)] = value

    pairs_of(z_ref, edge_ref, w_ref, put)


def adder(from_ref, to_ref):
    def put(p, value):
        at = slice(W * p, W * (p + 1))
        to_ref[:, at] = (from_ref[:, at] + value).astype(to_ref.dtype)

    return put


def proj_second_kernel(
    core_ref, r0_ref, r2_ref, m1_ref, m2_ref, m4_ref, edge_ref, turned_ref, early_ref, near_ref, out_ref, z_ref, w_ref
):
    @pl.when(core_ref[0] == 0)
    def _():
        fill(z_ref, blocks(r2_ref) + [r0_ref[...]])
        fill(w_ref, [m2_ref[...], m1_ref[...], m4_ref[...]])
        pairs_of(z_ref, edge_ref, w_ref, adder(early_ref, out_ref))
        near_ref[...] = jnp.zeros_like(near_ref)

    @pl.when(core_ref[0] != 0)
    def _():
        near_ref[...] = step(r2_ref[W:, :], turned_ref, edge_ref)


def finish(z_ref, edge_ref, w_ref, sum_ref, out_ref, stage_ref, sem):
    pieces = sem.shape[0]
    planes = edge_ref.shape[1] // W
    each = planes // pieces
    add = adder(sum_ref, stage_ref)
    copies = []

    def put(p, value):
        add(p, value)
        if (p + 1) % each == 0:
            at = pl.ds(W * (p + 1 - each), W * each)
            copies.append(pltpu.make_async_copy(stage_ref.at[:, at], out_ref.at[:, at], sem.at[p // each]))
            copies[-1].start()

    pairs_of(z_ref, edge_ref, w_ref, put)
    for copy in copies:
        copy.wait()


def proj_third_kernel(
    core_ref, corner_ref, r0_ref, r2_ref, m1_ref, m2_ref, m4_ref, m5_ref, edge_ref, early_ref, sum_ref, out_ref,
    z_ref, w_ref, stage_ref, sem,
):
    @pl.when(core_ref[0] == 0)
    def _():
        finish(corner_ref, edge_ref, m5_ref, early_ref, out_ref, stage_ref, sem)

    @pl.when(core_ref[0] != 0)
    def _():
        fill(z_ref, [m1_ref[...], m2_ref[...], m4_ref[...]])
        fill(w_ref, blocks(r2_ref)[::-1] + [r0_ref[...]])
        pairs_of(z_ref, edge_ref, w_ref, adder(early_ref, sum_ref))


def proj_last_kernel(core_ref, corner_ref, r3_ref, edge_ref, sum_ref, done_ref, out_ref, stage_ref, sem):
    @pl.when(core_ref[0] != 0)
    def _():
        finish(corner_ref, edge_ref, r3_ref, sum_ref, out_ref, stage_ref, sem)


def edge_kernel(
    core_ref, corner_ref, r0_ref, r1_ref, r2_ref, r3_ref, m1_ref, m2_ref, m3_ref, m4_ref, m5_ref, edge_ref, turned_ref,
    out_ref, grad_ref, z_ref, w_ref, sem,
):
    def halves(ref):
        return [ref.at[pl.ds(0, W)], ref.at[pl.ds(W, W)]]

    come = [r0_ref] + halves(r1_ref) + halves(r2_ref)
    mate = [m1_ref, m2_ref] + halves(m3_ref) + [m4_ref, m5_ref]

    def fetch(z_parts, w_parts):
        copies = []
        for n, part in enumerate(z_parts + w_parts):
            k = n % len(z_parts)
            to = z_ref if n < len(z_parts) else w_ref
            copies.append(pltpu.make_async_copy(part, to.at[pl.ds(W * k, W)], sem.at[n]))
        for copy in copies:
            copy.start()
        for copy in copies:
            copy.wait()

    @pl.when(core_ref[0] == 0)
    def _():
        fetch(mate[::-1], [corner_ref] + come)

    @pl.when(core_ref[0] != 0)
    def _():
        fetch([r3_ref] + come[::-1], [corner_ref] + mate[:5])

    def put(p, value):
        out_ref[:, W * p : W * (p + 1)] = value.T.astype(BF)

    pairs_of(z_ref, turned_ref, w_ref, put)
    grad_ref[...] = step(z_ref[:W, :], turned_ref, edge_ref).astype(F32).T.astype(BF)


def gather_kernel(parts_ref, out_ref):
    rows = parts_ref.shape[1]
    planes = parts_ref.shape[2] // W
    for p in range(planes):
        out_ref[pl.ds(p, rows, stride=planes), :] = jnp.sum(
            parts_ref[:, :, W * p : W * (p + 1)].astype(F32), axis=0
        )


def call(kernel, shapes, *args, scratch=(), sems=(), flops=0, far=(), free=(), far_outs=(), alias=None):
    def spec(n, arg):
        if n in far or n in free:
            return pl.BlockSpec(memory_space=pl.ANY)
        return pl.BlockSpec(memory_space=pltpu.SMEM if arg.dtype == jnp.int32 else pltpu.VMEM)

    moved = sum(arg.size * arg.dtype.itemsize for arg in args)
    single = len(shapes) == 1
    outs = [
        pltpu.HBM(shape, kind) if n in far_outs else jax.ShapeDtypeStruct(shape, kind)
        for n, (shape, kind) in enumerate(shapes)
    ]
    out_specs = [pl.BlockSpec(memory_space=pl.ANY if n in far_outs else pltpu.VMEM) for n in range(len(shapes))]
    in_specs = [spec(n, arg) for n, arg in enumerate(args)]
    args = [pltpu.with_memory_space_constraint(arg, pltpu.HBM) if n in far else arg for n, arg in enumerate(args)]
    return pl.pallas_call(
        kernel,
        out_shape=outs[0] if single else outs,
        in_specs=in_specs,
        out_specs=out_specs[0] if single else out_specs,
        scratch_shapes=[pltpu.VMEM(shape, kind) for shape, kind in scratch]
        + [pltpu.SemaphoreType.DMA((count,)) for count in sems],
        input_output_aliases=alias or {},
        compiler_params=pltpu.CompilerParams(vmem_limit_bytes=16 * 1024 * 1024),
        cost_estimate=pl.CostEstimate(flops=flops, bytes_accessed=moved, transcendentals=0),
    )(*args)


def shards(corners, edges, projectors, cotangent):
    corner = corners[0, 0]
    edge = edges[0, 0]
    projector = projectors[0]
    cot = cotangent[0, 0]
    width = edge.shape[1]
    rows = lax.axis_size("row")
    cols = lax.axis_size("col")
    core = (lax.axis_index("col") % 2).astype(jnp.int32).reshape(1)
    unit = 2 * W * W * width

    def send(value, to):
        pairs = [(i, to(i) % cols) for i in range(cols) if to(i) is not None]
        return lax.ppermute(value, "col", pairs)

    def swap(value):
        return send(value, lambda i: i ^ 1)

    def onward(value):
        return send(value, lambda i: i + 2 if i % 2 == 0 else i - 2)

    one, two = ((W, W), BF), ((2 * W, W), BF)
    whole, wide = ((W, width), BF), ((W, width), F32)

    def stacks(n):
        return [((n * W, W), BF), ((n * W, W), BF)]

    far_edge = swap(edge)
    turned, keep, first = call(
        start_kernel, [whole, one, one], core, projector, edge, corner, cot,
        scratch=[((width, W), BF), ((width, W), F32), ((W, width), BF), ((W, W), BF), ((W, W), BF)], sems=(4, 3),
        flops=2 * unit, far=(1, 2, 3, 4),
    )
    r0 = send(first, lambda i: i - 1 if i % 2 == 0 else i + 1)
    far_turned = swap(turned)
    ahead, mate_edge, mate_turned = call(
        ahead_kernel, [one, whole, whole], core, keep, far_edge, far_turned, sems=(2,), flops=2 * unit, free=(2, 3)
    )
    tensors = (edge, turned, mate_edge, mate_turned)
    near1, go1 = call(single_kernel, [one, two], core, r0, ahead, *tensors, flops=4 * unit)
    r1 = onward(go1)
    m1, m2 = swap(keep), swap(near1)
    near2, go2 = call(double_kernel, [two, two], core, r1, *tensors, m1, m2, flops=8 * unit)
    r2 = onward(go2)
    m3 = swap(near2)
    early = call(proj_first_kernel, [wide], core, r1, m3, edge, scratch=stacks(2), flops=0)
    near3, go3 = call(turn_back_kernel, [one, one], core, r2, *tensors, early, flops=4 * unit)
    r3 = send(go3, lambda i: None if i % 2 == 0 else i - 2)
    m4 = swap(near3)
    near4, early = call(
        proj_second_kernel, [one, wide], core, r0, r2, m1, m2, m4, edge, turned, early,
        scratch=stacks(3), flops=6 * unit, alias={8: 1},
    )
    m5 = send(near4, lambda i: None if i % 2 == 0 else i - 1)
    part, done = call(
        proj_third_kernel, [wide, whole], core, corner, r0, r2, m1, m2, m4, m5, edge, early,
        scratch=stacks(3) + [whole], sems=(6,), flops=6 * unit, far_outs=(1,), alias={9: 0},
    )
    done = call(
        proj_last_kernel, [whole], core, corner, r3, edge, part, done,
        scratch=[whole], sems=(6,), flops=2 * unit, free=(5,), far_outs=(0,), alias={5: 0},
    )
    share = W // rows
    parts = lax.all_to_all(done.reshape(rows, share, width), "row", 0, 0, tiled=True)
    edge_grad, corner_grad = call(
        edge_kernel, [whole, one], core, corner, r0, r1, r2, r3, m1, m2, m3, m4, m5, edge, turned,
        scratch=stacks(6), sems=(12,), flops=14 * unit, far=range(1, 11),
    )
    proj = call(gather_kernel, [((share * width // W, W), F32)], parts, flops=unit)
    return (corner_grad[None, None], edge_grad[None, None], proj[None])


def solution(mesh):
    placed = (
        P("row", "col", None, None),
        P("row", "col", None, None),
        P("col", None, None),
        P("row", "col", None, None),
    )
    return jax.shard_map(
        shards,
        mesh=mesh,
        in_specs=placed,
        out_specs=(P("row", "col", None, None), P("row", "col", None, None), P("col", "row", None)),
        check_vma=False,
    )
```

```python
import jax
import jax.numpy as jnp
from jax import lax
from jax.experimental import pallas as pl
from jax.experimental.pallas import tpu as pltpu
from jax.sharding import PartitionSpec as P


W = 128
BF = jnp.bfloat16
F32 = jnp.float32


def dot(a, b):
    return jnp.dot(a, b, preferred_element_type=F32)


def step(z, x_ref, y_ref):
    n = z.shape[0] // W
    total = None
    for t in range(x_ref.shape[1] // (2 * W)):
        cols = slice(2 * W * t, 2 * W * (t + 1))
        mid = dot(z, x_ref[:, cols]).astype(BF)
        tall = jnp.concatenate(
            [jnp.concatenate([mid[W * b : W * (b + 1), :W], mid[W * b : W * (b + 1), W:]], 0) for b in range(n)], 1
        )
        part = dot(y_ref[:, cols], tall)
        total = part if total is None else total + part
    return total.astype(BF)


def split(wide):
    return [wide[:, W * b : W * (b + 1)] for b in range(wide.shape[1] // W)]


def start_kernel(
    core_ref, proj_ref, edge_ref, corner_ref, cot_ref, turned_ref, keep_ref, send_ref,
    proj_in, wide_ref, edge_in, corner_in, cot_in, proj_sem, sem,
):
    pieces = proj_sem.shape[0]
    size = proj_ref.shape[0] // pieces
    loads = []
    for n in range(pieces):
        at = pl.ds(n * size, size)
        loads.append(pltpu.make_async_copy(proj_ref.at[at], proj_in.at[at], proj_sem.at[n]))
    others = [
        pltpu.make_async_copy(cot_ref, cot_in, sem.at[0]),
        pltpu.make_async_copy(corner_ref, corner_in, sem.at[1]),
        pltpu.make_async_copy(edge_ref, edge_in, sem.at[2]),
    ]
    for copy in loads + others:
        copy.start()
    for n, copy in enumerate(loads):
        copy.wait()
        at = slice(n * size, (n + 1) * size)
        wide_ref[at, :] = proj_in[at, :].astype(F32)
    planes = turned_ref.shape[1] // W
    for p in range(planes):
        turned_ref[:, W * p : W * (p + 1)] = wide_ref[pl.ds(p, W, stride=planes), :].T.astype(BF)
    for copy in others:
        copy.wait()
    cot_t = cot_in[...].astype(F32).T.astype(BF)
    moved = step(corner_in[...], edge_in, turned_ref)
    keep_ref[...] = jnp.where(core_ref[0] == 0, moved, cot_t)
    send_ref[...] = jnp.where(core_ref[0] == 0, cot_t, moved)


def by_role(core_ref, body, tensors):
    edge, turned, mate_edge, mate_turned = tensors

    @pl.when(core_ref[0] == 0)
    def _():
        body(edge, turned, mate_edge, mate_turned)

    @pl.when(core_ref[0] != 0)
    def _():
        body(turned, edge, mate_turned, mate_edge)


def ahead_kernel(core_ref, keep_ref, far_edge_ref, far_turned_ref, out_ref, mate_edge_ref, mate_turned_ref, sem):
    copies = [
        pltpu.make_async_copy(far_edge_ref, mate_edge_ref, sem.at[0]),
        pltpu.make_async_copy(far_turned_ref, mate_turned_ref, sem.at[1]),
    ]
    for copy in copies:
        copy.start()
    for copy in copies:
        copy.wait()

    def body(x1, y1, x2, y2):
        out_ref[...] = step(keep_ref[...], x2, y2)

    by_role(core_ref, body, (None, None, mate_edge_ref, mate_turned_ref))


def single_kernel(core_ref, come_ref, ahead_ref, e_ref, t_ref, me_ref, mt_ref, near_ref, far_ref):
    far_ref[:W, :] = ahead_ref[...]

    def body(x1, y1, x2, y2):
        near = step(come_ref[...], x1, y1)
        near_ref[...] = near
        far_ref[W:, :] = step(near, x2, y2)

    by_role(core_ref, body, (e_ref, t_ref, me_ref, mt_ref))


def double_kernel(core_ref, come_ref, e_ref, t_ref, me_ref, mt_ref, m1_ref, m2_ref, near_ref, far_ref):
    def body(x1, y1, x2, y2):
        near = jnp.concatenate(split(step(come_ref[...], x1, y1)), 0)
        near_ref[...] = near
        far_ref[...] = jnp.concatenate(split(step(near, x2, y2)), 0)

    by_role(core_ref, body, (e_ref, t_ref, me_ref, mt_ref))


def blocks(ref):
    return [ref[W * b : W * (b + 1), :] for b in range(ref.shape[0] // W)]


def fill(ref, parts):
    for b, part in enumerate(parts):
        ref[W * b : W * (b + 1), :] = part


def pairs_of(z_ref, x_ref, w_ref, put):
    n = z_ref.shape[0] // W
    for t in range(x_ref.shape[1] // (2 * W)):
        mid = dot(z_ref[...], x_ref[:, 2 * W * t : 2 * W * (t + 1)]).astype(BF)
        for half in range(2):
            flat = jnp.concatenate([mid[W * k : W * (k + 1), W * half : W * (half + 1)] for k in range(n)], 1)
            put(2 * t + half, dot(flat, w_ref[...]))


def proj_first_kernel(core_ref, r1_ref, m3_ref, edge_ref, out_ref, z_ref, w_ref):
    r1, m3 = blocks(r1_ref), blocks(m3_ref)

    @pl.when(core_ref[0] == 0)
    def _():
        fill(z_ref, r1)
        fill(w_ref, m3[::-1])

    @pl.when(core_ref[0] != 0)
    def _():
        fill(z_ref, m3)
        fill(w_ref, r1[::-1])

    def put(p, value):
        out_ref[:, W * p : W * (p + 1)] = value

    pairs_of(z_ref, edge_ref, w_ref, put)


def adder(from_ref, to_ref):
    def put(p, value):
        at = slice(W * p, W * (p + 1))
        to_ref[:, at] = (from_ref[:, at] + value).astype(to_ref.dtype)

    return put


def turn_back_kernel(
    core_ref, come_ref, m1_ref, m2_ref, e_ref, t_ref, me_ref, mt_ref, early_ref, same_ref, far_ref, out_ref,
    z_ref, w_ref,
):
    same_ref[...] = come_ref[...]

    @pl.when(core_ref[0] == 0)
    def _():
        fill(z_ref, blocks(come_ref))
        fill(w_ref, [m2_ref[...], m1_ref[...]])
        pairs_of(z_ref, e_ref, w_ref, adder(early_ref, out_ref))
        far_ref[...] = jnp.zeros_like(far_ref)

    @pl.when(core_ref[0] != 0)
    def _():
        far_ref[...] = step(step(come_ref[:W, :], t_ref, e_ref), mt_ref, me_ref)


def finish(z_ref, edge_ref, w_ref, sum_ref, out_ref, stage_ref, sem):
    pieces = sem.shape[0]
    planes = edge_ref.shape[1] // W
    each = planes // pieces
    add = adder(sum_ref, stage_ref)
    copies = []

    def put(p, value):
        add(p, value)
        if (p + 1) % each == 0:
            at = pl.ds(W * (p + 1 - each), W * each)
            copies.append(pltpu.make_async_copy(stage_ref.at[:, at], out_ref.at[:, at], sem.at[p // each]))
            copies[-1].start()

    pairs_of(z_ref, edge_ref, w_ref, put)
    for copy in copies:
        copy.wait()


def proj_third_kernel(
    core_ref, corner_ref, r0_ref, r2_ref, m1_ref, m2_ref, m4_ref, e_ref, me_ref, mt_ref, early_ref,
    near_ref, sum_ref, out_ref, z_ref, w_ref, stage_ref, sem,
):
    @pl.when(core_ref[0] == 0)
    def _():
        near = split(step(m4_ref[...], mt_ref, me_ref))
        fill(near_ref, near)
        fill(z_ref, [corner_ref[...], r0_ref[...]])
        fill(w_ref, near[::-1])
        two = slice(0, 2 * W)
        finish(z_ref.at[two], e_ref, w_ref.at[two], early_ref, out_ref, stage_ref, sem)

    @pl.when(core_ref[0] != 0)
    def _():
        near = step(m4_ref[:W, :], me_ref, mt_ref)
        fill(near_ref, [near, jnp.zeros_like(near)])
        fill(z_ref, [m1_ref[...], m2_ref[...], near])
        fill(w_ref, blocks(r2_ref)[::-1] + [r0_ref[...]])
        pairs_of(z_ref, e_ref, w_ref, adder(early_ref, sum_ref))


def proj_last_kernel(core_ref, corner_ref, r3_ref, edge_ref, sum_ref, done_ref, out_ref, stage_ref, sem):
    @pl.when(core_ref[0] != 0)
    def _():
        finish(corner_ref, edge_ref, r3_ref, sum_ref, out_ref, stage_ref, sem)


def edge_kernel(
    core_ref, corner_ref, r0_ref, r1_ref, r2_ref, r3_ref, m1_ref, m2_ref, m3_ref, near_ref, edge_ref, turned_ref,
    out_ref, grad_ref, z_ref, w_ref, sem,
):
    def halves(ref):
        return [ref.at[pl.ds(0, W)], ref.at[pl.ds(W, W)]]

    come = [r0_ref] + halves(r1_ref) + halves(r2_ref)
    mate = [m1_ref, m2_ref] + halves(m3_ref) + halves(near_ref)

    def fetch(z_parts, w_parts):
        copies = []
        for n, part in enumerate(z_parts + w_parts):
            k = n % len(z_parts)
            to = z_ref if n < len(z_parts) else w_ref
            copies.append(pltpu.make_async_copy(part, to.at[pl.ds(W * k, W)], sem.at[n]))
        for copy in copies:
            copy.start()
        for copy in copies:
            copy.wait()

    @pl.when(core_ref[0] == 0)
    def _():
        fetch(mate[::-1], [corner_ref] + come)

    @pl.when(core_ref[0] != 0)
    def _():
        fetch([r3_ref] + come[::-1], [corner_ref] + mate[:5])

    def put(p, value):
        out_ref[:, W * p : W * (p + 1)] = value.T.astype(BF)

    pairs_of(z_ref, turned_ref, w_ref, put)
    grad_ref[...] = step(z_ref[:W, :], turned_ref, edge_ref).astype(F32).T.astype(BF)


def gather_kernel(parts_ref, out_ref):
    rows = parts_ref.shape[1]
    planes = parts_ref.shape[2] // W
    for p in range(planes):
        out_ref[pl.ds(p, rows, stride=planes), :] = jnp.sum(
            parts_ref[:, :, W * p : W * (p + 1)].astype(F32), axis=0
        )


def call(kernel, shapes, *args, scratch=(), sems=(), flops=0, far=(), free=(), far_outs=(), alias=None):
    def spec(n, arg):
        if n in far or n in free:
            return pl.BlockSpec(memory_space=pl.ANY)
        return pl.BlockSpec(memory_space=pltpu.SMEM if arg.dtype == jnp.int32 else pltpu.VMEM)

    moved = sum(arg.size * arg.dtype.itemsize for arg in args)
    single = len(shapes) == 1
    outs = [
        pltpu.HBM(shape, kind) if n in far_outs else jax.ShapeDtypeStruct(shape, kind)
        for n, (shape, kind) in enumerate(shapes)
    ]
    out_specs = [pl.BlockSpec(memory_space=pl.ANY if n in far_outs else pltpu.VMEM) for n in range(len(shapes))]
    in_specs = [spec(n, arg) for n, arg in enumerate(args)]
    args = [pltpu.with_memory_space_constraint(arg, pltpu.HBM) if n in far else arg for n, arg in enumerate(args)]
    return pl.pallas_call(
        kernel,
        out_shape=outs[0] if single else outs,
        in_specs=in_specs,
        out_specs=out_specs[0] if single else out_specs,
        scratch_shapes=[pltpu.VMEM(shape, kind) for shape, kind in scratch]
        + [pltpu.SemaphoreType.DMA((count,)) for count in sems],
        input_output_aliases=alias or {},
        compiler_params=pltpu.CompilerParams(vmem_limit_bytes=16 * 1024 * 1024),
        cost_estimate=pl.CostEstimate(flops=flops, bytes_accessed=moved, transcendentals=0),
    )(*args)


def shards(corners, edges, projectors, cotangent):
    corner = corners[0, 0]
    edge = edges[0, 0]
    projector = projectors[0]
    cot = cotangent[0, 0]
    width = edge.shape[1]
    rows = lax.axis_size("row")
    cols = lax.axis_size("col")
    core = (lax.axis_index("col") % 2).astype(jnp.int32).reshape(1)
    unit = 2 * W * W * width

    def send(value, to):
        pairs = [(i, to(i) % cols) for i in range(cols) if to(i) is not None]
        return lax.ppermute(value, "col", pairs)

    def swap(value):
        return send(value, lambda i: i ^ 1)

    def onward(value):
        return send(value, lambda i: i + 2 if i % 2 == 0 else i - 2)

    one, two = ((W, W), BF), ((2 * W, W), BF)
    whole, wide = ((W, width), BF), ((W, width), F32)

    def stacks(n):
        return [((n * W, W), BF), ((n * W, W), BF)]

    far_edge = swap(edge)
    turned, keep, first = call(
        start_kernel, [whole, one, one], core, projector, edge, corner, cot,
        scratch=[((width, W), BF), ((width, W), F32), ((W, width), BF), ((W, W), BF), ((W, W), BF)], sems=(4, 3),
        flops=2 * unit, far=(1, 2, 3, 4),
    )
    r0 = send(first, lambda i: i - 1 if i % 2 == 0 else i + 1)
    far_turned = swap(turned)
    ahead, mate_edge, mate_turned = call(
        ahead_kernel, [one, whole, whole], core, keep, far_edge, far_turned, sems=(2,), flops=2 * unit, free=(2, 3)
    )
    tensors = (edge, turned, mate_edge, mate_turned)
    near1, go1 = call(single_kernel, [one, two], core, r0, ahead, *tensors, flops=4 * unit)
    r1 = onward(go1)
    m1, m2 = swap(keep), swap(near1)
    near2, go2 = call(double_kernel, [two, two], core, r1, *tensors, m1, m2, flops=8 * unit)
    r2 = onward(go2)
    m3 = swap(near2)
    early = call(proj_first_kernel, [wide], core, r1, m3, edge, scratch=stacks(2), flops=0)
    same, go3, early = call(
        turn_back_kernel, [two, one, wide], core, r2, m1, m2, *tensors, early,
        scratch=stacks(2), flops=4 * unit, alias={8: 2},
    )
    r3 = send(go3, lambda i: None if i % 2 == 0 else i - 2)
    m4 = swap(same)
    near3, part, done = call(
        proj_third_kernel, [two, wide, whole], core, corner, r0, r2, m1, m2, m4, edge, mate_edge, mate_turned, early,
        scratch=stacks(3) + [whole], sems=(6,), flops=6 * unit, far_outs=(2,), alias={10: 1},
    )
    done = call(
        proj_last_kernel, [whole], core, corner, r3, edge, part, done,
        scratch=[whole], sems=(6,), flops=2 * unit, free=(5,), far_outs=(0,), alias={5: 0},
    )
    share = W // rows
    parts = lax.all_to_all(done.reshape(rows, share, width), "row", 0, 0, tiled=True)
    edge_grad, corner_grad = call(
        edge_kernel, [whole, one], core, corner, r0, r1, r2, r3, m1, m2, m3, near3, edge, turned,
        scratch=stacks(6), sems=(12,), flops=14 * unit, far=range(1, 10),
    )
    proj = call(gather_kernel, [((share * width // W, W), F32)], parts, flops=unit)
    return (corner_grad[None, None], edge_grad[None, None], proj[None])


def solution(mesh):
    placed = (
        P("row", "col", None, None),
        P("row", "col", None, None),
        P("col", None, None),
        P("row", "col", None, None),
    )
    return jax.shard_map(
        shards,
        mesh=mesh,
        in_specs=placed,
        out_specs=(P("row", "col", None, None), P("row", "col", None, None), P("col", "row", None)),
        check_vma=False,
    )
```

```python
import jax
import jax.numpy as jnp
from jax import lax
from jax.experimental import pallas as pl
from jax.experimental.pallas import tpu as pltpu
from jax.sharding import PartitionSpec as P


W = 128
BF = jnp.bfloat16
F32 = jnp.float32


def dot(a, b):
    return jnp.dot(a, b, preferred_element_type=F32)


def step(z, x_ref, y_ref):
    n = z.shape[0] // W
    total = None
    for t in range(x_ref.shape[1] // (2 * W)):
        cols = slice(2 * W * t, 2 * W * (t + 1))
        mid = dot(z, x_ref[:, cols]).astype(BF)
        tall = jnp.concatenate(
            [jnp.concatenate([mid[W * b : W * (b + 1), :W], mid[W * b : W * (b + 1), W:]], 0) for b in range(n)], 1
        )
        part = dot(y_ref[:, cols], tall)
        total = part if total is None else total + part
    return total.astype(BF)


def split(wide):
    return [wide[:, W * b : W * (b + 1)] for b in range(wide.shape[1] // W)]


def start_kernel(
    core_ref, proj_ref, edge_in, corner_in, cot_ref, mate_cot_ref, turned_ref, edge_ref, corner_ref, last_ref, send_ref,
    proj_vmem, wide_ref, cot_vmem, proj_sem, sem,
):
    pieces = proj_sem.shape[0]
    size = proj_ref.shape[0] // pieces
    loads = []
    for n in range(pieces):
        at = pl.ds(n * size, size)
        loads.append(pltpu.make_async_copy(proj_ref.at[at], proj_vmem.at[at], proj_sem.at[n]))
    others = [
        pltpu.make_async_copy(cot_ref, cot_vmem.at[0], sem.at[0]),
        pltpu.make_async_copy(mate_cot_ref, cot_vmem.at[1], sem.at[1]),
        pltpu.make_async_copy(corner_in, corner_ref, sem.at[2]),
        pltpu.make_async_copy(edge_in, edge_ref, sem.at[3]),
    ]
    for copy in loads + others:
        copy.start()
    for n, copy in enumerate(loads):
        copy.wait()
        at = slice(n * size, (n + 1) * size)
        wide_ref[at, :] = proj_vmem[at, :].astype(F32)
    planes = turned_ref.shape[1] // W
    for p in range(planes):
        turned_ref[:, W * p : W * (p + 1)] = wide_ref[pl.ds(p, W, stride=planes), :].T.astype(BF)
    for copy in others:
        copy.wait()

    @pl.when(core_ref[0] == 0)
    def _():
        last = cot_vmem[1].astype(F32).T.astype(BF)
        last_ref[...] = last
        send_ref[:W, :] = cot_vmem[0].astype(F32).T.astype(BF)
        send_ref[W:, :] = step(last, turned_ref, edge_ref)

    @pl.when(core_ref[0] != 0)
    def _():
        last_ref[...] = corner_ref[...]
        moved = step(corner_ref[...], edge_ref, turned_ref)
        send_ref[:W, :] = moved
        send_ref[W:, :] = moved


def by_role(core_ref, body, tensors):
    edge, turned, mate_edge, mate_turned = tensors

    @pl.when(core_ref[0] == 0)
    def _():
        body(edge, turned, mate_edge, mate_turned)

    @pl.when(core_ref[0] != 0)
    def _():
        body(turned, edge, mate_turned, mate_edge)


def ahead_kernel(
    core_ref, corner_ref, e_ref, t_ref, far_edge_ref, far_turned_ref, keep_ref, out_ref, me_ref, mt_ref, sem
):
    copies = [
        pltpu.make_async_copy(far_edge_ref, me_ref, sem.at[0]),
        pltpu.make_async_copy(far_turned_ref, mt_ref, sem.at[1]),
    ]
    for copy in copies:
        copy.start()

    @pl.when(core_ref[0] == 0)
    def _():
        keep_ref[...] = step(corner_ref[...], e_ref, t_ref)

    for copy in copies:
        copy.wait()

    @pl.when(core_ref[0] == 0)
    def _():
        out_ref[...] = step(keep_ref[...], me_ref, mt_ref)

    @pl.when(core_ref[0] != 0)
    def _():
        keep_ref[...] = jnp.zeros_like(keep_ref)
        out_ref[...] = jnp.zeros_like(out_ref)


def first_kernel(
    core_ref, come_ref, corner_ref, keep_ref, ahead_ref, e_ref, t_ref, me_ref, mt_ref, v_ref, near_ref, far_ref
):
    @pl.when(core_ref[0] == 0)
    def _():
        near = step(come_ref[:W, :], e_ref, t_ref)
        fill(near_ref, [keep_ref[...], near])
        fill(far_ref, [ahead_ref[...], step(near, me_ref, mt_ref)])
        fill(v_ref, [corner_ref[...], come_ref[:W, :]])

    @pl.when(core_ref[0] != 0)
    def _():
        near = jnp.concatenate(split(step(come_ref[...], t_ref, e_ref)), 0)
        near_ref[...] = near
        fill(far_ref, split(step(near, mt_ref, me_ref)))
        v_ref[...] = come_ref[...]


def double_kernel(core_ref, come_ref, e_ref, t_ref, me_ref, mt_ref, m1_ref, near_ref, far_ref):
    def body(x1, y1, x2, y2):
        near = jnp.concatenate(split(step(come_ref[...], x1, y1)), 0)
        near_ref[...] = near
        far_ref[...] = jnp.concatenate(split(step(near, x2, y2)), 0)

    by_role(core_ref, body, (e_ref, t_ref, me_ref, mt_ref))


def blocks(ref):
    return [ref[W * b : W * (b + 1), :] for b in range(ref.shape[0] // W)]


def fill(ref, parts):
    for b, part in enumerate(parts):
        ref[W * b : W * (b + 1), :] = part


def pairs_of(z_ref, x_ref, w_ref, put):
    n = z_ref.shape[0] // W
    for t in range(x_ref.shape[1] // (2 * W)):
        mid = dot(z_ref[...], x_ref[:, 2 * W * t : 2 * W * (t + 1)]).astype(BF)
        for half in range(2):
            flat = jnp.concatenate([mid[W * k : W * (k + 1), W * half : W * (half + 1)] for k in range(n)], 1)
            put(2 * t + half, dot(flat, w_ref[...]))


def place(core_ref, z_ref, w_ref, v, u):
    @pl.when(core_ref[0] == 0)
    def _():
        fill(z_ref, v)
        fill(w_ref, u)

    @pl.when(core_ref[0] != 0)
    def _():
        fill(z_ref, u)
        fill(w_ref, v)


def proj_early_kernel(core_ref, v_ref, r1_ref, m1_ref, m2_ref, edge_ref, out_ref, z_ref, w_ref):
    place(core_ref, z_ref, w_ref, [v_ref[W:, :]] + blocks(r1_ref), blocks(m2_ref)[::-1] + [m1_ref[W:, :]])

    def put(p, value):
        out_ref[:, W * p : W * (p + 1)] = value

    pairs_of(z_ref, edge_ref, w_ref, put)


def pass_kernel(value_ref, after_ref, out_ref):
    out_ref[...] = value_ref[...]


def proj_late_kernel(core_ref, r2_ref, m1_ref, last_ref, edge_ref, early_ref, out_ref, z_ref, w_ref):
    place(core_ref, z_ref, w_ref, blocks(r2_ref), [m1_ref[:W, :], last_ref[...]])

    def put(p, value):
        at = slice(W * p, W * (p + 1))
        out_ref[:, at] = early_ref[:, at] + value

    pairs_of(z_ref, edge_ref, w_ref, put)


def proj_last_kernel(
    core_ref, v_ref, m3_ref, e_ref, me_ref, mt_ref, sum_ref, near_ref, out_ref, z_ref, w_ref, stage_ref, sem
):
    def body(x1, y1, x2, y2):
        near_ref[...] = step(m3_ref[:W, :], y2, x2)

    by_role(core_ref, body, (None, None, me_ref, mt_ref))
    place(core_ref, z_ref, w_ref, [v_ref[:W, :]], [near_ref[...]])
    pieces = sem.shape[0]
    each = e_ref.shape[1] // W // pieces
    copies = []

    def put(p, value):
        at = slice(W * p, W * (p + 1))
        stage_ref[:, at] = (sum_ref[:, at] + value).astype(BF)
        if (p + 1) % each == 0:
            at = pl.ds(W * (p + 1 - each), W * each)
            copies.append(pltpu.make_async_copy(stage_ref.at[:, at], out_ref.at[:, at], sem.at[p // each]))
            copies[-1].start()

    pairs_of(z_ref, e_ref, w_ref, put)
    for copy in copies:
        copy.wait()


def edge_kernel(
    core_ref, v_ref, r1_ref, r2_ref, near_ref, m2_ref, m1_ref, last_ref, edge_ref, turned_ref,
    out_ref, grad_ref, z_ref, w_ref, sem,
):
    def halves(ref):
        return [ref.at[pl.ds(0, W)], ref.at[pl.ds(W, W)]]

    v = halves(v_ref) + halves(r1_ref) + halves(r2_ref)
    u = [near_ref] + halves(m2_ref)[::-1] + halves(m1_ref)[::-1] + [last_ref]

    def fetch(z_parts, w_parts):
        copies = []
        for n, part in enumerate(z_parts + w_parts):
            k = n % len(z_parts)
            to = z_ref if n < len(z_parts) else w_ref
            copies.append(pltpu.make_async_copy(part, to.at[pl.ds(W * k, W)], sem.at[n]))
        for copy in copies:
            copy.start()
        for copy in copies:
            copy.wait()

    @pl.when(core_ref[0] == 0)
    def _():
        fetch(u, v)

    @pl.when(core_ref[0] != 0)
    def _():
        fetch(v[::-1], u[::-1])

    def put(p, value):
        out_ref[:, W * p : W * (p + 1)] = value.T.astype(BF)

    pairs_of(z_ref, turned_ref, w_ref, put)
    grad_ref[...] = step(z_ref[:W, :], turned_ref, edge_ref).astype(F32).T.astype(BF)


def gather_kernel(parts_ref, out_ref):
    rows = parts_ref.shape[1]
    planes = parts_ref.shape[2] // W
    for p in range(planes):
        out_ref[pl.ds(p, rows, stride=planes), :] = jnp.sum(
            parts_ref[:, :, W * p : W * (p + 1)].astype(F32), axis=0
        )


def call(kernel, shapes, *args, scratch=(), sems=(), flops=0, far=(), free=(), far_outs=(), alias=None):
    def spec(n, arg):
        if n in far or n in free:
            return pl.BlockSpec(memory_space=pl.ANY)
        return pl.BlockSpec(memory_space=pltpu.SMEM if arg.dtype == jnp.int32 else pltpu.VMEM)

    moved = sum(arg.size * arg.dtype.itemsize for arg in args)
    single = len(shapes) == 1
    outs = [
        pltpu.HBM(shape, kind) if n in far_outs else jax.ShapeDtypeStruct(shape, kind)
        for n, (shape, kind) in enumerate(shapes)
    ]
    out_specs = [pl.BlockSpec(memory_space=pl.ANY if n in far_outs else pltpu.VMEM) for n in range(len(shapes))]
    in_specs = [spec(n, arg) for n, arg in enumerate(args)]
    args = [pltpu.with_memory_space_constraint(arg, pltpu.HBM) if n in far else arg for n, arg in enumerate(args)]
    return pl.pallas_call(
        kernel,
        out_shape=outs[0] if single else outs,
        in_specs=in_specs,
        out_specs=out_specs[0] if single else out_specs,
        scratch_shapes=[pltpu.VMEM(shape, kind) for shape, kind in scratch]
        + [pltpu.SemaphoreType.DMA((count,)) for count in sems],
        input_output_aliases=alias or {},
        compiler_params=pltpu.CompilerParams(vmem_limit_bytes=16 * 1024 * 1024),
        cost_estimate=pl.CostEstimate(flops=flops, bytes_accessed=moved, transcendentals=0),
    )(*args)


def shards(corners, edges, projectors, cotangent):
    corner = corners[0, 0]
    edge = edges[0, 0]
    projector = projectors[0]
    cot = cotangent[0, 0]
    width = edge.shape[1]
    rows = lax.axis_size("row")
    cols = lax.axis_size("col")
    core = (lax.axis_index("col") % 2).astype(jnp.int32).reshape(1)
    unit = 2 * W * W * width

    def send(value, to):
        pairs = [(i, to(i) % cols) for i in range(cols) if to(i) is not None]
        return lax.ppermute(value, "col", pairs)

    def swap(value):
        return send(value, lambda i: i ^ 1)

    def onward(value):
        return send(value, lambda i: i + 2 if i % 2 == 0 else i - 2)

    one, two = ((W, W), BF), ((2 * W, W), BF)
    whole, wide = ((W, width), BF), ((W, width), F32)

    def stacks(n):
        return [((n * W, W), BF), ((n * W, W), BF)]

    mate_cot = swap(cot)
    far_edge = swap(edge)
    turned, edge, corner, u0, first = call(
        start_kernel, [whole, whole, one, one, two], core, projector, edge, corner, cot, mate_cot,
        scratch=[((width, W), BF), ((width, W), F32), ((2, W, W), BF)], sems=(4, 4), flops=3 * unit,
        far=(1, 2, 3, 4), free=(5,),
    )
    r0 = send(first, lambda i: i - 1 if i % 2 == 0 else i + 1)
    far_turned = swap(turned)
    keep, ahead, mate_edge, mate_turned = call(
        ahead_kernel, [one, one, whole, whole], core, corner, edge, turned, far_edge, far_turned,
        sems=(2,), flops=4 * unit, free=(4, 5),
    )
    tensors = (edge, turned, mate_edge, mate_turned)
    v, near1, go1 = call(first_kernel, [two, two, two], core, r0, corner, keep, ahead, *tensors, flops=4 * unit)
    r1 = onward(go1)
    m1 = swap(near1)
    near2, go2 = call(double_kernel, [two, two], core, r1, *tensors, m1, flops=8 * unit)
    r2 = onward(go2)
    m2 = swap(near2)
    early = call(proj_early_kernel, [wide], core, v, r1, m1, m2, edge, scratch=stacks(3), flops=6 * unit)
    r2 = call(pass_kernel, [two], r2, early, free=(1,))
    m3 = swap(r2)
    late = call(proj_late_kernel, [wide], core, r2, m1, u0, edge, early, scratch=stacks(2), flops=4 * unit, alias={5: 0})
    near3, done = call(
        proj_last_kernel, [one, whole], core, v, m3, edge, mate_edge, mate_turned, late,
        scratch=stacks(1) + [whole], sems=(6,), flops=4 * unit, far_outs=(1,),
    )
    share = W // rows
    parts = lax.all_to_all(done.reshape(rows, share, width), "row", 0, 0, tiled=True)
    edge_grad, corner_grad = call(
        edge_kernel, [whole, one], core, v, r1, r2, near3, m2, m1, u0, edge, turned,
        scratch=stacks(6), sems=(12,), flops=14 * unit, far=range(1, 8),
    )
    proj = call(gather_kernel, [((share * width // W, W), F32)], parts, flops=unit)
    return (corner_grad[None, None], edge_grad[None, None], proj[None])


def solution(mesh):
    placed = (
        P("row", "col", None, None),
        P("row", "col", None, None),
        P("col", None, None),
        P("row", "col", None, None),
    )
    return jax.shard_map(
        shards,
        mesh=mesh,
        in_specs=placed,
        out_specs=(P("row", "col", None, None), P("row", "col", None, None), P("col", "row", None)),
        check_vma=False,
    )
```

```python
import jax
import jax.numpy as jnp
from jax import lax
from jax.experimental import pallas as pl
from jax.experimental.pallas import tpu as pltpu
from jax.sharding import PartitionSpec as P


W = 128
H = W // 2
BF = jnp.bfloat16
F32 = jnp.float32


def dot(a, b):
    return jnp.dot(a, b, preferred_element_type=F32)


def step(z, x_ref, y_ref):
    n = z.shape[0] // W
    total = None
    for t in range(x_ref.shape[1] // (2 * W)):
        cols = slice(2 * W * t, 2 * W * (t + 1))
        mid = dot(z, x_ref[:, cols]).astype(BF)
        tall = jnp.concatenate(
            [jnp.concatenate([mid[W * b : W * (b + 1), :W], mid[W * b : W * (b + 1), W:]], 0) for b in range(n)], 1
        )
        part = dot(y_ref[:, cols], tall)
        total = part if total is None else total + part
    return total.astype(BF)


def split(wide):
    return [wide[:, W * b : W * (b + 1)] for b in range(wide.shape[1] // W)]


def start_kernel(
    core_ref, proj_ref, edge_in, corner_in, cot_ref, mate_cot_ref, turned_ref, edge_ref, corner_ref, last_ref, send_ref,
    proj_vmem, wide_ref, cot_vmem, proj_sem, sem,
):
    pieces = proj_sem.shape[0]
    size = proj_ref.shape[0] // pieces
    loads = []
    for n in range(pieces):
        at = pl.ds(n * size, size)
        loads.append(pltpu.make_async_copy(proj_ref.at[at], proj_vmem.at[at], proj_sem.at[n]))
    others = [
        pltpu.make_async_copy(cot_ref, cot_vmem.at[0], sem.at[0]),
        pltpu.make_async_copy(mate_cot_ref, cot_vmem.at[1], sem.at[1]),
        pltpu.make_async_copy(corner_in, corner_ref, sem.at[2]),
        pltpu.make_async_copy(edge_in, edge_ref, sem.at[3]),
    ]
    for copy in loads + others:
        copy.start()
    for n, copy in enumerate(loads):
        copy.wait()
        at = slice(n * size, (n + 1) * size)
        wide_ref[at, :] = proj_vmem[at, :].astype(F32)
    planes = turned_ref.shape[1] // W
    for p in range(planes):
        turned_ref[:, W * p : W * (p + 1)] = wide_ref[pl.ds(p, W, stride=planes), :].T.astype(BF)
    for copy in others:
        copy.wait()

    @pl.when(core_ref[0] == 0)
    def _():
        last = cot_vmem[1].astype(F32).T.astype(BF)
        last_ref[...] = last
        send_ref[:W, :] = cot_vmem[0].astype(F32).T.astype(BF)
        send_ref[W:, :] = step(last, turned_ref, edge_ref)

    @pl.when(core_ref[0] != 0)
    def _():
        last_ref[...] = corner_ref[...]
        moved = step(corner_ref[...], edge_ref, turned_ref)
        send_ref[:W, :] = moved
        send_ref[W:, :] = moved


def by_role(core_ref, body, tensors):
    edge, turned, mate_edge, mate_turned = tensors

    @pl.when(core_ref[0] == 0)
    def _():
        body(edge, turned, mate_edge, mate_turned)

    @pl.when(core_ref[0] != 0)
    def _():
        body(turned, edge, mate_turned, mate_edge)


def ahead_kernel(
    core_ref, corner_ref, e_ref, t_ref, far_edge_ref, far_turned_ref, keep_ref, out_ref, me_ref, mt_ref, sem
):
    copies = [
        pltpu.make_async_copy(far_edge_ref, me_ref, sem.at[0]),
        pltpu.make_async_copy(far_turned_ref, mt_ref, sem.at[1]),
    ]
    for copy in copies:
        copy.start()

    @pl.when(core_ref[0] == 0)
    def _():
        keep_ref[...] = step(corner_ref[...], e_ref, t_ref)

    for copy in copies:
        copy.wait()

    @pl.when(core_ref[0] == 0)
    def _():
        out_ref[...] = step(keep_ref[...], me_ref, mt_ref)

    @pl.when(core_ref[0] != 0)
    def _():
        keep_ref[...] = jnp.zeros_like(keep_ref)
        out_ref[...] = jnp.zeros_like(out_ref)


def first_kernel(
    core_ref, come_ref, corner_ref, keep_ref, ahead_ref, e_ref, t_ref, me_ref, mt_ref, v_ref, near_ref, far_ref
):
    @pl.when(core_ref[0] == 0)
    def _():
        near = step(come_ref[:W, :], e_ref, t_ref)
        fill(near_ref, [keep_ref[...], near])
        fill(far_ref, [ahead_ref[...], step(near, me_ref, mt_ref)])
        fill(v_ref, [corner_ref[...], come_ref[:W, :]])

    @pl.when(core_ref[0] != 0)
    def _():
        near = jnp.concatenate(split(step(come_ref[...], t_ref, e_ref)), 0)
        near_ref[...] = near
        fill(far_ref, split(step(near, mt_ref, me_ref)))
        v_ref[...] = come_ref[...]


def double_kernel(core_ref, come_ref, e_ref, t_ref, me_ref, mt_ref, m1_ref, near_ref, far_ref):
    def body(x1, y1, x2, y2):
        near = jnp.concatenate(split(step(come_ref[...], x1, y1)), 0)
        near_ref[...] = near
        far_ref[...] = jnp.concatenate(split(step(near, x2, y2)), 0)

    by_role(core_ref, body, (e_ref, t_ref, me_ref, mt_ref))


def blocks(ref):
    return [ref[W * b : W * (b + 1), :] for b in range(ref.shape[0] // W)]


def fill(ref, parts):
    for b, part in enumerate(parts):
        ref[W * b : W * (b + 1), :] = part


def pairs_of(z_ref, x_ref, w_ref, put):
    n = z_ref.shape[0] // W
    for t in range(x_ref.shape[1] // (2 * W)):
        mid = dot(z_ref[...], x_ref[:, 2 * W * t : 2 * W * (t + 1)]).astype(BF)
        for half in range(2):
            flat = jnp.concatenate([mid[W * k : W * (k + 1), W * half : W * (half + 1)] for k in range(n)], 1)
            put(2 * t + half, dot(flat, w_ref[...]))


def block(ref, k):
    return ref, W * k


def place(core_ref, z_ref, w_ref, v, u):
    def put(corners, adjoints):
        for n, ((c_ref, c_at), (a_ref, a_at)) in enumerate(zip(corners, adjoints)):
            at = pl.multiple_of(c_at + H * core_ref[1], H)
            z_ref[H * n : H * (n + 1), :] = c_ref[pl.ds(at, H), :]
            w_ref[W * n : W * (n + 1), :] = a_ref[a_at : a_at + W, :]

    @pl.when(core_ref[0] == 0)
    def _():
        put(v, u)

    @pl.when(core_ref[0] != 0)
    def _():
        put(u, v)


def terms_of(z_ref, x_ref, w_ref, put):
    n = z_ref.shape[0] // H
    for t in range(x_ref.shape[1] // (2 * W)):
        mid = dot(z_ref[...], x_ref[:, 2 * W * t : 2 * W * (t + 1)]).astype(BF)
        flat = jnp.concatenate(
            [
                jnp.concatenate([mid[H * k : H * (k + 1), W * half : W * (half + 1)] for k in range(n)], 1)
                for half in range(2)
            ],
            0,
        )
        value = dot(flat, w_ref[...])
        put(2 * t, value[:H, :])
        put(2 * t + 1, value[H:, :])


def adder(from_ref, to_ref):
    def put(p, value):
        at = slice(W * p, W * (p + 1))
        to_ref[:, at] = from_ref[:, at] + value

    return put


def pack_kernel(v_ref, m1_ref, last_ref, out_ref):
    out_ref[: 2 * W, :] = v_ref[...]
    out_ref[2 * W : 4 * W, :] = m1_ref[...]
    out_ref[4 * W :, :] = last_ref[...]


def middle(v_ref, r1_ref, m1_ref, m2_ref):
    v = [block(v_ref, 1), block(r1_ref, 0), block(r1_ref, 1)]
    return v, [block(m2_ref, 1), block(m2_ref, 0), block(m1_ref, 1)]


def proj_early_kernel(core_ref, v_ref, r1_ref, m1_ref, m2_ref, edge_ref, out_ref, pack_ref, z_ref, w_ref):
    place(core_ref, z_ref, w_ref, *middle(v_ref, r1_ref, m1_ref, m2_ref))
    pack_ref[: 2 * W, :] = r1_ref[...]
    pack_ref[2 * W :, :] = m2_ref[...]

    def put(p, value):
        out_ref[:, W * p : W * (p + 1)] = value

    terms_of(z_ref, edge_ref, w_ref, put)


def pass_kernel(value_ref, after_ref, out_ref):
    out_ref[...] = value_ref[...]


def proj_late_kernel(core_ref, r2_ref, m1_ref, last_ref, edge_ref, early_ref, out_ref, z_ref, w_ref):
    place(
        core_ref, z_ref, w_ref, [block(r2_ref, 0), block(r2_ref, 1)], [block(m1_ref, 0), block(last_ref, 0)]
    )
    terms_of(z_ref, edge_ref, w_ref, adder(early_ref, out_ref))


def near_kernel(core_ref, m3_ref, me_ref, mt_ref, after_ref, near_ref):
    def body(x1, y1, x2, y2):
        near_ref[...] = step(m3_ref[:W, :], y2, x2)

    by_role(core_ref, body, (None, None, me_ref, mt_ref))


def proj_other_kernel(
    core_ref, v_ref, near_ref, pack1_ref, pack2_ref, r2_ref, edge_ref, other_edge_ref, sum_ref, out_ref,
    z1_ref, w1_ref, z_ref, w_ref,
):
    place(core_ref, z1_ref, w1_ref, [block(v_ref, 0)], [block(near_ref, 0)])
    terms_of(z1_ref, edge_ref, w1_ref, adder(sum_ref, out_ref))
    v = [block(pack1_ref, 1), block(pack2_ref, 0), block(pack2_ref, 1), block(r2_ref, 0), block(r2_ref, 1)]
    u = [block(pack2_ref, 3), block(pack2_ref, 2), block(pack1_ref, 3), block(pack1_ref, 2), block(pack1_ref, 4)]
    place(core_ref, z_ref, w_ref, v, u)
    terms_of(z_ref, other_edge_ref, w_ref, adder(out_ref, out_ref))


def proj_last_kernel(
    core_ref, pack1_ref, near_ref, other_edge_ref, sum_ref, out_ref, z_ref, w_ref, stage_ref, sem
):
    place(core_ref, z_ref, w_ref, [block(pack1_ref, 0)], [block(near_ref, 0)])
    pieces = sem.shape[0]
    each = stage_ref.shape[1] // W // pieces
    copies = []

    def put(p, value):
        at = slice(W * p, W * (p + 1))
        stage_ref[:, at] = (sum_ref[:, at] + value).astype(BF)
        if (p + 1) % each == 0:
            at = pl.ds(W * (p + 1 - each), W * each)
            copies.append(pltpu.make_async_copy(stage_ref.at[:, at], out_ref.at[:, at], sem.at[p // each]))
            copies[-1].start()

    terms_of(z_ref, other_edge_ref, w_ref, put)
    for copy in copies:
        copy.wait()


def edge_kernel(
    core_ref, v_ref, r1_ref, r2_ref, near_ref, m2_ref, m1_ref, last_ref, edge_ref, turned_ref,
    out_ref, grad_ref, z_ref, w_ref, sem,
):
    def halves(ref):
        return [ref.at[pl.ds(0, W)], ref.at[pl.ds(W, W)]]

    v = halves(v_ref) + halves(r1_ref) + halves(r2_ref)
    u = [near_ref] + halves(m2_ref)[::-1] + halves(m1_ref)[::-1] + [last_ref]

    def fetch(z_parts, w_parts):
        copies = []
        for n, part in enumerate(z_parts + w_parts):
            k = n % len(z_parts)
            to = z_ref if n < len(z_parts) else w_ref
            copies.append(pltpu.make_async_copy(part, to.at[pl.ds(W * k, W)], sem.at[n]))
        for copy in copies:
            copy.start()
        for copy in copies:
            copy.wait()

    @pl.when(core_ref[0] == 0)
    def _():
        fetch(u, v)

    @pl.when(core_ref[0] != 0)
    def _():
        fetch(v[::-1], u[::-1])

    def put(p, value):
        out_ref[:, W * p : W * (p + 1)] = value.T.astype(BF)

    pairs_of(z_ref, turned_ref, w_ref, put)
    grad_ref[...] = step(z_ref[:W, :], turned_ref, edge_ref).astype(F32).T.astype(BF)


def gather_kernel(parts_ref, out_ref):
    rows = parts_ref.shape[1]
    planes = parts_ref.shape[2] // W
    for p in range(planes):
        out_ref[pl.ds(p, rows, stride=planes), :] = jnp.sum(
            parts_ref[:, :, W * p : W * (p + 1)].astype(F32), axis=0
        )


def call(kernel, shapes, *args, scratch=(), sems=(), flops=0, far=(), free=(), far_outs=(), alias=None):
    def spec(n, arg):
        if n in far or n in free:
            return pl.BlockSpec(memory_space=pl.ANY)
        return pl.BlockSpec(memory_space=pltpu.SMEM if arg.dtype == jnp.int32 else pltpu.VMEM)

    moved = sum(arg.size * arg.dtype.itemsize for arg in args)
    single = len(shapes) == 1
    outs = [
        pltpu.HBM(shape, kind) if n in far_outs else jax.ShapeDtypeStruct(shape, kind)
        for n, (shape, kind) in enumerate(shapes)
    ]
    out_specs = [pl.BlockSpec(memory_space=pl.ANY if n in far_outs else pltpu.VMEM) for n in range(len(shapes))]
    in_specs = [spec(n, arg) for n, arg in enumerate(args)]
    args = [pltpu.with_memory_space_constraint(arg, pltpu.HBM) if n in far else arg for n, arg in enumerate(args)]
    return pl.pallas_call(
        kernel,
        out_shape=outs[0] if single else outs,
        in_specs=in_specs,
        out_specs=out_specs[0] if single else out_specs,
        scratch_shapes=[pltpu.VMEM(shape, kind) for shape, kind in scratch]
        + [pltpu.SemaphoreType.DMA((count,)) for count in sems],
        input_output_aliases=alias or {},
        compiler_params=pltpu.CompilerParams(vmem_limit_bytes=16 * 1024 * 1024),
        cost_estimate=pl.CostEstimate(flops=flops, bytes_accessed=moved, transcendentals=0),
    )(*args)


def shards(corners, edges, projectors, cotangent):
    corner = corners[0, 0]
    edge = edges[0, 0]
    projector = projectors[0]
    cot = cotangent[0, 0]
    width = edge.shape[1]
    rows = lax.axis_size("row")
    cols = lax.axis_size("col")
    across = rows // 2
    core = jnp.stack([lax.axis_index("col") % 2, lax.axis_index("row") // across]).astype(jnp.int32)
    unit = 2 * W * W * width

    def send(value, to):
        pairs = [(i, to(i) % cols) for i in range(cols) if to(i) is not None]
        return lax.ppermute(value, "col", pairs)

    def swap(value):
        return send(value, lambda i: i ^ 1)

    def trade(value):
        return lax.ppermute(value, "row", [(i, (i + across) % rows) for i in range(rows)])

    def onward(value):
        return send(value, lambda i: i + 2 if i % 2 == 0 else i - 2)

    one, two = ((W, W), BF), ((2 * W, W), BF)
    half = ((H, width), F32)
    whole = ((W, width), BF)

    def stacks(n):
        return [((n * W, W), BF), ((n * W, W), BF)]

    mate_cot = swap(cot)
    far_edge = swap(edge)
    other_edge = trade(edge)
    turned, edge, corner, u0, first = call(
        start_kernel, [whole, whole, one, one, two], core, projector, edge, corner, cot, mate_cot,
        scratch=[((width, W), BF), ((width, W), F32), ((2, W, W), BF)], sems=(4, 4), flops=3 * unit,
        far=(1, 2, 3, 4, 5),
    )
    r0 = send(first, lambda i: i - 1 if i % 2 == 0 else i + 1)
    far_turned = swap(turned)
    keep, ahead, mate_edge, mate_turned = call(
        ahead_kernel, [one, one, whole, whole], core, corner, edge, turned, far_edge, far_turned,
        sems=(2,), flops=4 * unit, free=(4, 5),
    )
    tensors = (edge, turned, mate_edge, mate_turned)
    v, near1, go1 = call(first_kernel, [two, two, two], core, r0, corner, keep, ahead, *tensors, flops=4 * unit)
    r1 = onward(go1)
    m1 = swap(near1)
    pack1 = call(pack_kernel, [((5 * W, W), BF)], v, m1, u0)
    near2, go2 = call(double_kernel, [two, two], core, r1, *tensors, pack1, flops=8 * unit)
    other1 = trade(pack1)
    r2 = onward(go2)
    m2 = swap(near2)

    def halves(n):
        return [((n * H, W), BF), ((n * W, W), BF)]

    early, pack2 = call(
        proj_early_kernel, [half, ((4 * W, W), BF)], core, v, r1, m1, m2, edge, scratch=halves(3), flops=3 * unit
    )
    other2 = trade(pack2)
    r2 = call(pass_kernel, [two], r2, early, free=(1,))
    m3 = swap(r2)
    other3 = trade(r2)
    late = call(proj_late_kernel, [half], core, r2, m1, u0, edge, early, scratch=halves(2), flops=2 * unit, alias={5: 0})
    near3 = call(near_kernel, [one], core, m3, mate_edge, mate_turned, late, flops=2 * unit, free=(4,))
    other4 = trade(near3)
    late = call(
        proj_other_kernel, [half], core, v, near3, other1, other2, other3, edge, other_edge, late,
        scratch=halves(1) + halves(5), flops=6 * unit, alias={8: 0},
    )
    done = call(
        proj_last_kernel, [((H, width), BF)], core, other1, other4, other_edge, late,
        scratch=halves(1) + [((H, width), BF)], sems=(6,), flops=unit, far_outs=(0,),
    )
    share = W // rows
    groups = [list(range(across)), list(range(across, rows))]
    parts = lax.all_to_all(
        done.reshape(across, share, width), "row", 0, 0, tiled=True, axis_index_groups=groups
    )
    edge_grad, corner_grad = call(
        edge_kernel, [whole, one], core, v, r1, r2, near3, m2, m1, u0, edge, turned,
        scratch=stacks(6), sems=(12,), flops=14 * unit, far=(1, 2, 3, 5, 6, 7),
    )
    proj = call(gather_kernel, [((share * width // W, W), F32)], parts, flops=unit)
    return (corner_grad[None, None], edge_grad[None, None], proj[None])


def solution(mesh):
    placed = (
        P("row", "col", None, None),
        P("row", "col", None, None),
        P("col", None, None),
        P("row", "col", None, None),
    )
    return jax.shard_map(
        shards,
        mesh=mesh,
        in_specs=placed,
        out_specs=(P("row", "col", None, None), P("row", "col", None, None), P("col", "row", None)),
        check_vma=False,
    )
```

```python
import jax
import jax.numpy as jnp
from jax import lax
from jax.experimental import pallas as pl
from jax.experimental.pallas import tpu as pltpu
from jax.sharding import PartitionSpec as P


W = 128
PIECES = 3
BF = jnp.bfloat16
F32 = jnp.float32


def dot(a, b):
    return jnp.dot(a, b, preferred_element_type=F32)


def step(z, x_ref, y_ref):
    n = z.shape[0] // W
    total = None
    for t in range(x_ref.shape[1] // (2 * W)):
        cols = slice(2 * W * t, 2 * W * (t + 1))
        mid = dot(z, x_ref[:, cols]).astype(BF)
        tall = jnp.concatenate(
            [jnp.concatenate([mid[W * b : W * (b + 1), :W], mid[W * b : W * (b + 1), W:]], 0) for b in range(n)], 1
        )
        part = dot(y_ref[:, cols], tall)
        total = part if total is None else total + part
    return total.astype(BF)


def split(wide):
    return [wide[:, W * b : W * (b + 1)] for b in range(wide.shape[1] // W)]


def start_kernel(
    core_ref, proj_ref, edge_in, corner_in, cot_ref, mate_cot_ref, turned_ref, edge_ref, corner_ref, last_ref, send_ref, mine_ref, *rest,
):
    *give, proj_vmem, wide_ref, cot_vmem, proj_sem, sem = rest
    pieces = proj_sem.shape[0]
    size = proj_ref.shape[0] // pieces
    loads = []
    for n in range(pieces):
        at = pl.ds(n * size, size)
        loads.append(pltpu.make_async_copy(proj_ref.at[at], proj_vmem.at[at], proj_sem.at[n]))
    others = [
        pltpu.make_async_copy(cot_ref, cot_vmem.at[0], sem.at[0]),
        pltpu.make_async_copy(mate_cot_ref, cot_vmem.at[1], sem.at[1]),
        pltpu.make_async_copy(corner_in, corner_ref, sem.at[2]),
        pltpu.make_async_copy(edge_in, edge_ref, sem.at[3]),
    ]
    for copy in loads + others:
        copy.start()
    for n, copy in enumerate(loads):
        copy.wait()
        at = slice(n * size, (n + 1) * size)
        wide_ref[at, :] = proj_vmem[at, :].astype(F32)
    planes = turned_ref.shape[1] // W
    for p in range(planes):
        turned_ref[:, W * p : W * (p + 1)] = wide_ref[pl.ds(p, W, stride=planes), :].T.astype(BF)
    for copy in others:
        copy.wait()

    part = mine_ref.shape[1]
    mine_ref[...] = edge_ref[:, pl.ds(pl.multiple_of(part * core_ref[1], W), part)]
    for n, ref in enumerate(give):
        at = part * (1 - core_ref[1]) + n * ref.shape[1]
        ref[...] = edge_ref[:, pl.ds(pl.multiple_of(at, W), ref.shape[1])]

    @pl.when(core_ref[0] == 0)
    def _():
        last = cot_vmem[1].astype(F32).T.astype(BF)
        last_ref[...] = last
        send_ref[:W, :] = cot_vmem[0].astype(F32).T.astype(BF)
        send_ref[W:, :] = step(last, turned_ref, edge_ref)

    @pl.when(core_ref[0] != 0)
    def _():
        last_ref[...] = corner_ref[...]
        moved = step(corner_ref[...], edge_ref, turned_ref)
        send_ref[:W, :] = moved
        send_ref[W:, :] = moved


def by_role(core_ref, body, tensors):
    edge, turned, mate_edge, mate_turned = tensors

    @pl.when(core_ref[0] == 0)
    def _():
        body(edge, turned, mate_edge, mate_turned)

    @pl.when(core_ref[0] != 0)
    def _():
        body(turned, edge, mate_turned, mate_edge)


def ahead_kernel(
    core_ref, corner_ref, e_ref, t_ref, far_edge_ref, far_turned_ref, keep_ref, out_ref, me_ref, mt_ref, sem
):
    copies = [
        pltpu.make_async_copy(far_edge_ref, me_ref, sem.at[0]),
        pltpu.make_async_copy(far_turned_ref, mt_ref, sem.at[1]),
    ]
    for copy in copies:
        copy.start()

    @pl.when(core_ref[0] == 0)
    def _():
        keep_ref[...] = step(corner_ref[...], e_ref, t_ref)

    for copy in copies:
        copy.wait()

    @pl.when(core_ref[0] == 0)
    def _():
        out_ref[...] = step(keep_ref[...], me_ref, mt_ref)

    @pl.when(core_ref[0] != 0)
    def _():
        keep_ref[...] = jnp.zeros_like(keep_ref)
        out_ref[...] = jnp.zeros_like(out_ref)


def first_kernel(
    core_ref, come_ref, corner_ref, keep_ref, ahead_ref, e_ref, t_ref, me_ref, mt_ref, v_ref, near_ref, far_ref
):
    @pl.when(core_ref[0] == 0)
    def _():
        near = step(come_ref[:W, :], e_ref, t_ref)
        fill(near_ref, [keep_ref[...], near])
        fill(far_ref, [ahead_ref[...], step(near, me_ref, mt_ref)])
        fill(v_ref, [corner_ref[...], come_ref[:W, :]])

    @pl.when(core_ref[0] != 0)
    def _():
        near = jnp.concatenate(split(step(come_ref[...], t_ref, e_ref)), 0)
        near_ref[...] = near
        fill(far_ref, split(step(near, mt_ref, me_ref)))
        v_ref[...] = come_ref[...]


def double_kernel(core_ref, come_ref, e_ref, t_ref, me_ref, mt_ref, m1_ref, near_ref, far_ref):
    def body(x1, y1, x2, y2):
        near = jnp.concatenate(split(step(come_ref[...], x1, y1)), 0)
        near_ref[...] = near
        far_ref[...] = jnp.concatenate(split(step(near, x2, y2)), 0)

    by_role(core_ref, body, (e_ref, t_ref, me_ref, mt_ref))


def blocks(ref):
    return [ref[W * b : W * (b + 1), :] for b in range(ref.shape[0] // W)]


def fill(ref, parts):
    for b, part in enumerate(parts):
        ref[W * b : W * (b + 1), :] = part


def pairs_of(z_ref, x_ref, w_ref, put):
    n = z_ref.shape[0] // W
    for t in range(x_ref.shape[1] // (2 * W)):
        mid = dot(z_ref[...], x_ref[:, 2 * W * t : 2 * W * (t + 1)]).astype(BF)
        for half in range(2):
            flat = jnp.concatenate([mid[W * k : W * (k + 1), W * half : W * (half + 1)] for k in range(n)], 1)
            put(2 * t + half, dot(flat, w_ref[...]))


def block(ref, k):
    return ref, W * k


def place(core_ref, z_ref, w_ref, v, u):
    def put(corners, adjoints):
        for n, ((c_ref, c_at), (a_ref, a_at)) in enumerate(zip(corners, adjoints)):
            z_ref[W * n : W * (n + 1), :] = c_ref[c_at : c_at + W, :]
            w_ref[W * n : W * (n + 1), :] = a_ref[a_at : a_at + W, :]

    @pl.when(core_ref[0] == 0)
    def _():
        put(v, u)

    @pl.when(core_ref[0] != 0)
    def _():
        put(u, v)


def adder(from_ref, to_ref, start=0):
    def put(p, value):
        at = slice(start + W * p, start + W * (p + 1))
        to_ref[:, at] = from_ref[:, at] + value

    return put


def pack_kernel(v_ref, m1_ref, last_ref, out_ref):
    out_ref[: 2 * W, :] = v_ref[...]
    out_ref[2 * W : 4 * W, :] = m1_ref[...]
    out_ref[4 * W :, :] = last_ref[...]


def middle(v_ref, r1_ref, m1_ref, m2_ref):
    v = [block(v_ref, 1), block(r1_ref, 0), block(r1_ref, 1)]
    return v, [block(m2_ref, 1), block(m2_ref, 0), block(m1_ref, 1)]


def proj_early_kernel(core_ref, v_ref, r1_ref, m1_ref, m2_ref, edge_ref, out_ref, pack_ref, z_ref, w_ref):
    place(core_ref, z_ref, w_ref, *middle(v_ref, r1_ref, m1_ref, m2_ref))
    pack_ref[: 2 * W, :] = r1_ref[...]
    pack_ref[2 * W :, :] = m2_ref[...]

    def put(p, value):
        out_ref[:, W * p : W * (p + 1)] = value

    pairs_of(z_ref, edge_ref, w_ref, put)


def pass_kernel(value_ref, after_ref, out_ref):
    out_ref[...] = value_ref[...]


def proj_late_kernel(core_ref, r2_ref, m1_ref, last_ref, edge_ref, early_ref, out_ref, z_ref, w_ref):
    place(
        core_ref, z_ref, w_ref, [block(r2_ref, 0), block(r2_ref, 1)], [block(m1_ref, 0), block(last_ref, 0)]
    )
    pairs_of(z_ref, edge_ref, w_ref, adder(early_ref, out_ref))


def near_kernel(core_ref, m3_ref, me_ref, mt_ref, after_ref, near_ref):
    def body(x1, y1, x2, y2):
        near_ref[...] = step(m3_ref[:W, :], y2, x2)

    by_role(core_ref, body, (None, None, me_ref, mt_ref))


def proj_other_kernel(
    core_ref, v_ref, near_ref, pack1_ref, pack2_ref, r2_ref, mine_ref, sum_ref, *rest
):
    *other_refs, out_ref, z1_ref, w1_ref, z_ref, w_ref = rest
    place(core_ref, z1_ref, w1_ref, [block(v_ref, 0)], [block(near_ref, 0)])
    pairs_of(z1_ref, mine_ref, w1_ref, adder(sum_ref, out_ref))
    v = [block(pack1_ref, 1), block(pack2_ref, 0), block(pack2_ref, 1), block(r2_ref, 0), block(r2_ref, 1)]
    u = [block(pack2_ref, 3), block(pack2_ref, 2), block(pack1_ref, 3), block(pack1_ref, 2), block(pack1_ref, 4)]
    place(core_ref, z_ref, w_ref, v, u)
    for n, ref in enumerate(other_refs):
        pairs_of(z_ref, ref, w_ref, adder(out_ref, out_ref, n * ref.shape[1]))


def proj_last_kernel(core_ref, pack1_ref, near_ref, sum_ref, *rest):
    *other_refs, out_ref, z_ref, w_ref, stage_ref, sem = rest
    place(core_ref, z_ref, w_ref, [block(pack1_ref, 0)], [block(near_ref, 0)])
    copies = []
    for n, ref in enumerate(other_refs):

        def put(p, value, at=n * ref.shape[1]):
            at = slice(at + W * p, at + W * (p + 1))
            stage_ref[:, at] = (sum_ref[:, at] + value).astype(BF)

        pairs_of(z_ref, ref, w_ref, put)
        at = pl.ds(n * ref.shape[1], ref.shape[1])
        copies.append(pltpu.make_async_copy(stage_ref.at[:, at], out_ref.at[:, at], sem.at[n]))
        copies[-1].start()
    for copy in copies:
        copy.wait()


def edge_kernel(
    core_ref, v_ref, r1_ref, r2_ref, near_ref, m2_ref, m1_ref, last_ref, edge_ref, turned_ref,
    out_ref, grad_ref, z_ref, w_ref, sem,
):
    def halves(ref):
        return [ref.at[pl.ds(0, W)], ref.at[pl.ds(W, W)]]

    v = halves(v_ref) + halves(r1_ref) + halves(r2_ref)
    u = [near_ref] + halves(m2_ref)[::-1] + halves(m1_ref)[::-1] + [last_ref]

    def fetch(z_parts, w_parts):
        copies = []
        for n, part in enumerate(z_parts + w_parts):
            k = n % len(z_parts)
            to = z_ref if n < len(z_parts) else w_ref
            copies.append(pltpu.make_async_copy(part, to.at[pl.ds(W * k, W)], sem.at[n]))
        for copy in copies:
            copy.start()
        for copy in copies:
            copy.wait()

    @pl.when(core_ref[0] == 0)
    def _():
        fetch(u, v)

    @pl.when(core_ref[0] != 0)
    def _():
        fetch(v[::-1], u[::-1])

    def put(p, value):
        out_ref[:, W * p : W * (p + 1)] = value.T.astype(BF)

    pairs_of(z_ref, turned_ref, w_ref, put)
    grad_ref[...] = step(z_ref[:W, :], turned_ref, edge_ref).astype(F32).T.astype(BF)


def gather_kernel(parts_ref, out_ref):
    senders, rows, part = parts_ref.shape
    planes = 2 * part // W
    for p in range(planes):
        half, at = divmod(W * p, part)
        these = slice(senders // 2 * half, senders // 2 * (half + 1))
        out_ref[pl.ds(p, rows, stride=planes), :] = jnp.sum(parts_ref[these, :, at : at + W].astype(F32), axis=0)


def call(kernel, shapes, *args, scratch=(), sems=(), flops=0, far=(), free=(), far_outs=(), alias=None):
    def spec(n, arg):
        if n in far or n in free:
            return pl.BlockSpec(memory_space=pl.ANY)
        return pl.BlockSpec(memory_space=pltpu.SMEM if arg.dtype == jnp.int32 else pltpu.VMEM)

    moved = sum(arg.size * arg.dtype.itemsize for arg in args)
    single = len(shapes) == 1
    outs = [
        pltpu.HBM(shape, kind) if n in far_outs else jax.ShapeDtypeStruct(shape, kind)
        for n, (shape, kind) in enumerate(shapes)
    ]
    out_specs = [pl.BlockSpec(memory_space=pl.ANY if n in far_outs else pltpu.VMEM) for n in range(len(shapes))]
    in_specs = [spec(n, arg) for n, arg in enumerate(args)]
    args = [pltpu.with_memory_space_constraint(arg, pltpu.HBM) if n in far else arg for n, arg in enumerate(args)]
    return pl.pallas_call(
        kernel,
        out_shape=outs[0] if single else outs,
        in_specs=in_specs,
        out_specs=out_specs[0] if single else out_specs,
        scratch_shapes=[pltpu.VMEM(shape, kind) for shape, kind in scratch]
        + [pltpu.SemaphoreType.DMA((count,)) for count in sems],
        input_output_aliases=alias or {},
        compiler_params=pltpu.CompilerParams(vmem_limit_bytes=16 * 1024 * 1024),
        cost_estimate=pl.CostEstimate(flops=flops, bytes_accessed=moved, transcendentals=0),
    )(*args)


def shards(corners, edges, projectors, cotangent):
    corner = corners[0, 0]
    edge = edges[0, 0]
    projector = projectors[0]
    cot = cotangent[0, 0]
    width = edge.shape[1]
    rows = lax.axis_size("row")
    cols = lax.axis_size("col")
    across = rows // 2
    core = jnp.stack([lax.axis_index("col") % 2, lax.axis_index("row") // across]).astype(jnp.int32)
    unit = 2 * W * W * width

    def send(value, to):
        pairs = [(i, to(i) % cols) for i in range(cols) if to(i) is not None]
        return lax.ppermute(value, "col", pairs)

    def swap(value):
        return send(value, lambda i: i ^ 1)

    def trade(value):
        return lax.ppermute(value, "row", [(i, (i + across) % rows) for i in range(rows)])

    def onward(value):
        return send(value, lambda i: i + 2 if i % 2 == 0 else i - 2)

    one, two = ((W, W), BF), ((2 * W, W), BF)
    half_width = width // 2
    half = ((W, half_width), F32)
    piece = ((W, half_width // PIECES), BF)
    whole = ((W, width), BF)

    def stacks(n):
        return [((n * W, W), BF), ((n * W, W), BF)]

    mate_cot = swap(cot)
    far_edge = swap(edge)
    turned, edge, corner, u0, first, mine, *give = call(
        start_kernel, [whole, whole, one, one, two, ((W, half_width), BF)] + [piece] * PIECES, core, projector, edge, corner, cot, mate_cot,
        scratch=[((width, W), BF), ((width, W), F32), ((2, W, W), BF)], sems=(4, 4), flops=3 * unit,
        far=(1, 2, 3, 4, 5),
    )
    r0 = send(first, lambda i: i - 1 if i % 2 == 0 else i + 1)
    far_turned = swap(turned)
    other_edge = [trade(part) for part in give]
    keep, ahead, mate_edge, mate_turned = call(
        ahead_kernel, [one, one, whole, whole], core, corner, edge, turned, far_edge, far_turned,
        sems=(2,), flops=4 * unit, free=(4, 5),
    )
    tensors = (edge, turned, mate_edge, mate_turned)
    v, near1, go1 = call(first_kernel, [two, two, two], core, r0, corner, keep, ahead, *tensors, flops=4 * unit)
    r1 = onward(go1)
    m1 = swap(near1)
    pack1 = call(pack_kernel, [((5 * W, W), BF)], v, m1, u0)
    near2, go2 = call(double_kernel, [two, two], core, r1, *tensors, pack1, flops=8 * unit)
    other1 = trade(pack1)
    r2 = onward(go2)
    m2 = swap(near2)

    def halves(n):
        return [((n * W, W), BF), ((n * W, W), BF)]

    early, pack2 = call(
        proj_early_kernel, [half, ((4 * W, W), BF)], core, v, r1, m1, m2, mine, scratch=halves(3), flops=3 * unit
    )
    other2 = trade(pack2)
    r2 = call(pass_kernel, [two], r2, early, free=(1,))
    m3 = swap(r2)
    other3 = trade(r2)
    late = call(proj_late_kernel, [half], core, r2, m1, u0, mine, early, scratch=halves(2), flops=2 * unit, alias={5: 0})
    near3 = call(near_kernel, [one], core, m3, mate_edge, mate_turned, late, flops=2 * unit, free=(4,))
    other4 = trade(near3)
    late = call(
        proj_other_kernel, [half], core, v, near3, other1, other2, other3, mine, late, *other_edge,
        scratch=halves(1) + halves(5), flops=6 * unit, alias={7: 0},
    )
    done = call(
        proj_last_kernel, [((W, half_width), BF)], core, other1, other4, late, *other_edge,
        scratch=halves(1) + [((W, half_width), BF)], sems=(PIECES,), flops=unit, far_outs=(0,),
    )
    share = W // rows
    parts = lax.all_to_all(done.reshape(rows, share, half_width), "row", 0, 0, tiled=True)
    edge_grad, corner_grad = call(
        edge_kernel, [whole, one], core, v, r1, r2, near3, m2, m1, u0, edge, turned,
        scratch=stacks(6), sems=(12,), flops=14 * unit, far=(1, 2, 3, 5, 6, 7),
    )
    proj = call(gather_kernel, [((share * width // W, W), F32)], parts, flops=unit)
    return (corner_grad[None, None], edge_grad[None, None], proj[None])


def solution(mesh):
    placed = (
        P("row", "col", None, None),
        P("row", "col", None, None),
        P("col", None, None),
        P("row", "col", None, None),
    )
    return jax.shard_map(
        shards,
        mesh=mesh,
        in_specs=placed,
        out_specs=(P("row", "col", None, None), P("row", "col", None, None), P("col", "row", None)),
        check_vma=False,
    )
```

```python
import jax
import jax.numpy as jnp
from jax import lax
from jax.experimental import pallas as pl
from jax.experimental.pallas import tpu as pltpu
from jax.sharding import PartitionSpec as P


W = 128
BF = jnp.bfloat16
F32 = jnp.float32


def dot(a, b):
    return jnp.dot(a, b, preferred_element_type=F32)


def step(z, x_ref, y_ref):
    n = z.shape[0] // W
    total = None
    for t in range(x_ref.shape[1] // (2 * W)):
        cols = slice(2 * W * t, 2 * W * (t + 1))
        mid = dot(z, x_ref[:, cols]).astype(BF)
        tall = jnp.concatenate(
            [jnp.concatenate([mid[W * b : W * (b + 1), :W], mid[W * b : W * (b + 1), W:]], 0) for b in range(n)], 1
        )
        part = dot(y_ref[:, cols], tall)
        total = part if total is None else total + part
    return total.astype(BF)


def split(wide):
    return [wide[:, W * b : W * (b + 1)] for b in range(wide.shape[1] // W)]


def turn_kernel(
    proj_ref, edge_in, corner_in, cot_ref, turned_ref, edge_ref, corner_ref, cot_t_ref,
    proj_vmem, wide_ref, cot_vmem, proj_sem, sem,
):
    pieces = proj_sem.shape[0]
    size = proj_ref.shape[0] // pieces
    loads = []
    for n in range(pieces):
        at = pl.ds(n * size, size)
        loads.append(pltpu.make_async_copy(proj_ref.at[at], proj_vmem.at[at], proj_sem.at[n]))
    others = [
        pltpu.make_async_copy(cot_ref, cot_vmem, sem.at[0]),
        pltpu.make_async_copy(corner_in, corner_ref, sem.at[1]),
        pltpu.make_async_copy(edge_in, edge_ref, sem.at[2]),
    ]
    for copy in loads + others:
        copy.start()
    for n, copy in enumerate(loads):
        copy.wait()
        at = slice(n * size, (n + 1) * size)
        wide_ref[at, :] = proj_vmem[at, :].astype(F32)
    planes = turned_ref.shape[1] // W
    for p in range(planes):
        turned_ref[:, W * p : W * (p + 1)] = wide_ref[pl.ds(p, W, stride=planes), :].T.astype(BF)
    for copy in others:
        copy.wait()
    cot_t_ref[...] = cot_vmem[...].astype(F32).T.astype(BF)


def own_kernel(core_ref, corner_ref, cot_t_ref, mate_cot_ref, edge_ref, turned_ref, last_ref, send_ref, same_ref):
    @pl.when(core_ref[0] == 0)
    def _():
        last = mate_cot_ref[...].astype(F32).T.astype(BF)
        last_ref[...] = last
        send_ref[:W, :] = cot_t_ref[...]
        send_ref[W:, :] = step(last, turned_ref, edge_ref)

    @pl.when(core_ref[0] != 0)
    def _():
        last_ref[...] = corner_ref[...]
        moved = step(corner_ref[...], edge_ref, turned_ref)
        send_ref[:W, :] = moved
        send_ref[W:, :] = moved


def by_role(core_ref, body, tensors):
    edge, turned, mate_edge, mate_turned = tensors

    @pl.when(core_ref[0] == 0)
    def _():
        body(edge, turned, mate_edge, mate_turned)

    @pl.when(core_ref[0] != 0)
    def _():
        body(turned, edge, mate_turned, mate_edge)


def ahead_kernel(
    core_ref, corner_ref, e_ref, t_ref, far_edge_ref, far_turned_ref, keep_ref, out_ref, me_ref, mt_ref, sem
):
    copies = [
        pltpu.make_async_copy(far_edge_ref, me_ref, sem.at[0]),
        pltpu.make_async_copy(far_turned_ref, mt_ref, sem.at[1]),
    ]
    for copy in copies:
        copy.start()

    @pl.when(core_ref[0] == 0)
    def _():
        keep_ref[...] = step(corner_ref[...], e_ref, t_ref)

    for copy in copies:
        copy.wait()

    @pl.when(core_ref[0] == 0)
    def _():
        out_ref[...] = step(keep_ref[...], me_ref, mt_ref)

    @pl.when(core_ref[0] != 0)
    def _():
        keep_ref[...] = jnp.zeros_like(keep_ref)
        out_ref[...] = jnp.zeros_like(out_ref)


def first_kernel(
    core_ref, come_ref, corner_ref, keep_ref, ahead_ref, e_ref, t_ref, me_ref, mt_ref, v_ref, near_ref, far_ref
):
    @pl.when(core_ref[0] == 0)
    def _():
        near = step(come_ref[:W, :], e_ref, t_ref)
        fill(near_ref, [keep_ref[...], near])
        fill(far_ref, [ahead_ref[...], step(near, me_ref, mt_ref)])
        fill(v_ref, [corner_ref[...], come_ref[:W, :]])

    @pl.when(core_ref[0] != 0)
    def _():
        near = jnp.concatenate(split(step(come_ref[...], t_ref, e_ref)), 0)
        near_ref[...] = near
        fill(far_ref, split(step(near, mt_ref, me_ref)))
        v_ref[...] = come_ref[...]


def double_kernel(core_ref, come_ref, e_ref, t_ref, me_ref, mt_ref, m1_ref, near_ref, far_ref):
    def body(x1, y1, x2, y2):
        near = jnp.concatenate(split(step(come_ref[...], x1, y1)), 0)
        near_ref[...] = near
        far_ref[...] = jnp.concatenate(split(step(near, x2, y2)), 0)

    by_role(core_ref, body, (e_ref, t_ref, me_ref, mt_ref))


def blocks(ref):
    return [ref[W * b : W * (b + 1), :] for b in range(ref.shape[0] // W)]


def fill(ref, parts):
    for b, part in enumerate(parts):
        ref[W * b : W * (b + 1), :] = part


def pairs_of(z_ref, x_ref, w_ref, put):
    n = z_ref.shape[0] // W
    for t in range(x_ref.shape[1] // (2 * W)):
        mid = dot(z_ref[...], x_ref[:, 2 * W * t : 2 * W * (t + 1)]).astype(BF)
        for half in range(2):
            flat = jnp.concatenate([mid[W * k : W * (k + 1), W * half : W * (half + 1)] for k in range(n)], 1)
            put(2 * t + half, dot(flat, w_ref[...]))


def place(core_ref, z_ref, w_ref, v, u):
    @pl.when(core_ref[0] == 0)
    def _():
        fill(z_ref, v)
        fill(w_ref, u)

    @pl.when(core_ref[0] != 0)
    def _():
        fill(z_ref, u)
        fill(w_ref, v)


def proj_early_kernel(core_ref, v_ref, r1_ref, m1_ref, m2_ref, edge_ref, out_ref, z_ref, w_ref):
    place(core_ref, z_ref, w_ref, [v_ref[W:, :]] + blocks(r1_ref), blocks(m2_ref)[::-1] + [m1_ref[W:, :]])

    def put(p, value):
        out_ref[:, W * p : W * (p + 1)] = value

    pairs_of(z_ref, edge_ref, w_ref, put)


def pass_kernel(value_ref, after_ref, out_ref):
    out_ref[...] = value_ref[...]


def proj_late_kernel(core_ref, r2_ref, m1_ref, last_ref, edge_ref, early_ref, out_ref, z_ref, w_ref):
    place(core_ref, z_ref, w_ref, blocks(r2_ref), [m1_ref[:W, :], last_ref[...]])

    def put(p, value):
        at = slice(W * p, W * (p + 1))
        out_ref[:, at] = early_ref[:, at] + value

    pairs_of(z_ref, edge_ref, w_ref, put)


def proj_last_kernel(
    core_ref, v_ref, m3_ref, e_ref, me_ref, mt_ref, sum_ref, near_out_ref, out_ref,
    near_ref, z_ref, w_ref, stage_ref, sem, near_sem,
):
    def body(x1, y1, x2, y2):
        near_ref[...] = step(m3_ref[:W, :], y2, x2)

    by_role(core_ref, body, (None, None, me_ref, mt_ref))
    copies = [pltpu.make_async_copy(near_ref, near_out_ref, near_sem.at[0])]
    copies[0].start()
    place(core_ref, z_ref, w_ref, [v_ref[:W, :]], [near_ref[...]])
    pieces = sem.shape[0]
    each = e_ref.shape[1] // W // pieces

    def put(p, value):
        at = slice(W * p, W * (p + 1))
        stage_ref[:, at] = (sum_ref[:, at] + value).astype(BF)
        if (p + 1) % each == 0:
            at = pl.ds(W * (p + 1 - each), W * each)
            copies.append(pltpu.make_async_copy(stage_ref.at[:, at], out_ref.at[:, at], sem.at[p // each]))
            copies[-1].start()

    pairs_of(z_ref, e_ref, w_ref, put)
    for copy in copies:
        copy.wait()


def edge_kernel(
    core_ref, v_ref, r1_ref, r2_ref, near_ref, m2_ref, m1_ref, last_ref, edge_ref, turned_ref,
    out_ref, grad_ref, z_ref, w_ref, sem,
):
    def halves(ref):
        return [ref.at[pl.ds(0, W)], ref.at[pl.ds(W, W)]]

    v = halves(v_ref) + halves(r1_ref) + halves(r2_ref)
    u = [near_ref] + halves(m2_ref)[::-1] + halves(m1_ref)[::-1] + [last_ref]

    def fetch(z_parts, w_parts):
        copies = []
        for n, part in enumerate(z_parts + w_parts):
            k = n % len(z_parts)
            to = z_ref if n < len(z_parts) else w_ref
            copies.append(pltpu.make_async_copy(part, to.at[pl.ds(W * k, W)], sem.at[n]))
        for copy in copies:
            copy.start()
        for copy in copies:
            copy.wait()

    @pl.when(core_ref[0] == 0)
    def _():
        fetch(u, v)

    @pl.when(core_ref[0] != 0)
    def _():
        fetch(v[::-1], u[::-1])

    def put(p, value):
        out_ref[:, W * p : W * (p + 1)] = value.T.astype(BF)

    pairs_of(z_ref, turned_ref, w_ref, put)
    grad_ref[...] = step(z_ref[:W, :], turned_ref, edge_ref).astype(F32).T.astype(BF)


def gather_kernel(parts_ref, out_ref):
    rows = parts_ref.shape[1]
    planes = parts_ref.shape[2] // W
    for p in range(planes):
        out_ref[pl.ds(p, rows, stride=planes), :] = jnp.sum(
            parts_ref[:, :, W * p : W * (p + 1)].astype(F32), axis=0
        )


def call(kernel, shapes, *args, scratch=(), sems=(), flops=0, far=(), free=(), far_outs=(), alias=None):
    def spec(n, arg):
        if n in far or n in free:
            return pl.BlockSpec(memory_space=pl.ANY)
        return pl.BlockSpec(memory_space=pltpu.SMEM if arg.dtype == jnp.int32 else pltpu.VMEM)

    moved = sum(arg.size * arg.dtype.itemsize for arg in args)
    single = len(shapes) == 1
    outs = [
        pltpu.HBM(shape, kind) if n in far_outs else jax.ShapeDtypeStruct(shape, kind)
        for n, (shape, kind) in enumerate(shapes)
    ]
    out_specs = [pl.BlockSpec(memory_space=pl.ANY if n in far_outs else pltpu.VMEM) for n in range(len(shapes))]
    in_specs = [spec(n, arg) for n, arg in enumerate(args)]
    args = [pltpu.with_memory_space_constraint(arg, pltpu.HBM) if n in far else arg for n, arg in enumerate(args)]
    return pl.pallas_call(
        kernel,
        out_shape=outs[0] if single else outs,
        in_specs=in_specs,
        out_specs=out_specs[0] if single else out_specs,
        scratch_shapes=[pltpu.VMEM(shape, kind) for shape, kind in scratch]
        + [pltpu.SemaphoreType.DMA((count,)) for count in sems],
        input_output_aliases=alias or {},
        compiler_params=pltpu.CompilerParams(vmem_limit_bytes=16 * 1024 * 1024),
        cost_estimate=pl.CostEstimate(flops=flops, bytes_accessed=moved, transcendentals=0),
    )(*args)


def shards(corners, edges, projectors, cotangent):
    corner = corners[0, 0]
    edge = edges[0, 0]
    projector = projectors[0]
    cot = cotangent[0, 0]
    width = edge.shape[1]
    rows = lax.axis_size("row")
    cols = lax.axis_size("col")
    core = (lax.axis_index("col") % 2).astype(jnp.int32).reshape(1)
    unit = 2 * W * W * width

    def send(value, to):
        pairs = [(i, to(i) % cols) for i in range(cols) if to(i) is not None]
        return lax.ppermute(value, "col", pairs)

    def swap(value):
        return send(value, lambda i: i ^ 1)

    def onward(value):
        return send(value, lambda i: i + 2 if i % 2 == 0 else i - 2)

    one, two = ((W, W), BF), ((2 * W, W), BF)
    whole, wide = ((W, width), BF), ((W, width), F32)

    def stacks(n):
        return [((n * W, W), BF), ((n * W, W), BF)]

    mate_cot = swap(cot)
    far_edge = swap(edge)
    turned, edge, corner, cot_t = call(
        turn_kernel, [whole, whole, one, one], projector, edge, corner, cot,
        scratch=[((width, W), BF), ((width, W), F32), ((W, W), BF)], sems=(4, 3), flops=unit, far=(0, 1, 2, 3),
    )
    u0, first, turned = call(
        own_kernel, [one, two, whole], core, corner, cot_t, mate_cot, edge, turned, flops=2 * unit, alias={5: 2}
    )
    r0 = send(first, lambda i: i - 1 if i % 2 == 0 else i + 1)
    far_turned = swap(turned)
    keep, ahead, mate_edge, mate_turned = call(
        ahead_kernel, [one, one, whole, whole], core, corner, edge, turned, far_edge, far_turned,
        sems=(2,), flops=4 * unit, free=(4, 5),
    )
    tensors = (edge, turned, mate_edge, mate_turned)
    v, near1, go1 = call(first_kernel, [two, two, two], core, r0, corner, keep, ahead, *tensors, flops=4 * unit)
    r1 = onward(go1)
    m1 = swap(near1)
    near2, go2 = call(double_kernel, [two, two], core, r1, *tensors, m1, flops=8 * unit)
    r2 = onward(go2)
    m2 = swap(near2)
    early = call(proj_early_kernel, [wide], core, v, r1, m1, m2, edge, scratch=stacks(3), flops=6 * unit)
    r2 = call(pass_kernel, [two], r2, early, free=(1,))
    m3 = swap(r2)
    late = call(proj_late_kernel, [wide], core, r2, m1, u0, edge, early, scratch=stacks(2), flops=4 * unit, alias={5: 0})
    near3, done = call(
        proj_last_kernel, [one, whole], core, v, m3, edge, mate_edge, mate_turned, late,
        scratch=[one] + stacks(1) + [whole], sems=(18, 1), flops=4 * unit, far_outs=(0, 1),
    )
    share = W // rows
    parts = lax.all_to_all(done.reshape(rows, share, width), "row", 0, 0, tiled=True)
    edge_grad, corner_grad = call(
        edge_kernel, [whole, one], core, v, r1, r2, near3, m2, m1, u0, edge, turned,
        scratch=stacks(6), sems=(12,), flops=14 * unit, far=range(1, 8),
    )
    proj = call(gather_kernel, [((share * width // W, W), F32)], parts, flops=unit)
    return (corner_grad[None, None], edge_grad[None, None], proj[None])


def solution(mesh):
    placed = (
        P("row", "col", None, None),
        P("row", "col", None, None),
        P("col", None, None),
        P("row", "col", None, None),
    )
    return jax.shard_map(
        shards,
        mesh=mesh,
        in_specs=placed,
        out_specs=(P("row", "col", None, None), P("row", "col", None, None), P("col", "row", None)),
        check_vma=False,
    )
```

```python
import jax
import jax.numpy as jnp
from jax import lax
from jax.experimental import pallas as pl
from jax.experimental.pallas import tpu as pltpu
from jax.sharding import PartitionSpec as P


W = 128
BF = jnp.bfloat16
F32 = jnp.float32


def dot(a, b):
    return jnp.dot(a, b, preferred_element_type=F32)


def step(z, x_ref, y_ref):
    n = z.shape[0] // W
    total = None
    for t in range(x_ref.shape[1] // (2 * W)):
        cols = slice(2 * W * t, 2 * W * (t + 1))
        mid = dot(z, x_ref[:, cols]).astype(BF)
        tall = jnp.concatenate(
            [jnp.concatenate([mid[W * b : W * (b + 1), :W], mid[W * b : W * (b + 1), W:]], 0) for b in range(n)], 1
        )
        part = dot(y_ref[:, cols], tall)
        total = part if total is None else total + part
    return total.astype(BF)


def split(wide):
    return [wide[:, W * b : W * (b + 1)] for b in range(wide.shape[1] // W)]


def turn_kernel(
    proj_ref, edge_in, corner_in, cot_ref, turned_ref, edge_ref, corner_ref, cot_t_ref,
    proj_vmem, wide_ref, cot_vmem, proj_sem, sem,
):
    pieces = proj_sem.shape[0]
    size = proj_ref.shape[0] // pieces
    loads = []
    for n in range(pieces):
        at = pl.ds(n * size, size)
        loads.append(pltpu.make_async_copy(proj_ref.at[at], proj_vmem.at[at], proj_sem.at[n]))
    others = [
        pltpu.make_async_copy(cot_ref, cot_vmem, sem.at[0]),
        pltpu.make_async_copy(corner_in, corner_ref, sem.at[1]),
        pltpu.make_async_copy(edge_in, edge_ref, sem.at[2]),
    ]
    for copy in loads + others:
        copy.start()
    for n, copy in enumerate(loads):
        copy.wait()
        at = slice(n * size, (n + 1) * size)
        wide_ref[at, :] = proj_vmem[at, :].astype(F32)
    planes = turned_ref.shape[1] // W
    for p in range(planes):
        turned_ref[:, W * p : W * (p + 1)] = wide_ref[pl.ds(p, W, stride=planes), :].T.astype(BF)
    for copy in others:
        copy.wait()
    cot_t_ref[...] = cot_vmem[...].astype(F32).T.astype(BF)


def own_kernel(core_ref, corner_ref, cot_t_ref, mate_cot_ref, edge_ref, turned_ref, last_ref, send_ref, same_ref):
    @pl.when(core_ref[0] == 0)
    def _():
        last = mate_cot_ref[...].astype(F32).T.astype(BF)
        last_ref[...] = last
        send_ref[:W, :] = cot_t_ref[...]
        send_ref[W:, :] = step(last, turned_ref, edge_ref)

    @pl.when(core_ref[0] != 0)
    def _():
        last_ref[...] = corner_ref[...]
        moved = step(corner_ref[...], edge_ref, turned_ref)
        send_ref[:W, :] = moved
        send_ref[W:, :] = moved


def by_role(core_ref, body, tensors):
    edge, turned, mate_edge, mate_turned = tensors

    @pl.when(core_ref[0] == 0)
    def _():
        body(edge, turned, mate_edge, mate_turned)

    @pl.when(core_ref[0] != 0)
    def _():
        body(turned, edge, mate_turned, mate_edge)


def ahead_kernel(
    core_ref, corner_ref, e_ref, t_ref, far_edge_ref, far_turned_ref, keep_ref, out_ref, me_ref, mt_ref, sem
):
    copies = [
        pltpu.make_async_copy(far_edge_ref, me_ref, sem.at[0]),
        pltpu.make_async_copy(far_turned_ref, mt_ref, sem.at[1]),
    ]
    for copy in copies:
        copy.start()

    @pl.when(core_ref[0] == 0)
    def _():
        keep_ref[...] = step(corner_ref[...], e_ref, t_ref)

    for copy in copies:
        copy.wait()

    @pl.when(core_ref[0] == 0)
    def _():
        out_ref[...] = step(keep_ref[...], me_ref, mt_ref)

    @pl.when(core_ref[0] != 0)
    def _():
        keep_ref[...] = jnp.zeros_like(keep_ref)
        out_ref[...] = jnp.zeros_like(out_ref)


def first_kernel(
    core_ref, come_ref, corner_ref, keep_ref, ahead_ref, e_ref, t_ref, me_ref, mt_ref, v_ref, near_ref, far_ref
):
    @pl.when(core_ref[0] == 0)
    def _():
        near = step(come_ref[:W, :], e_ref, t_ref)
        fill(near_ref, [keep_ref[...], near])
        fill(far_ref, [ahead_ref[...], step(near, me_ref, mt_ref)])
        fill(v_ref, [corner_ref[...], come_ref[:W, :]])

    @pl.when(core_ref[0] != 0)
    def _():
        near = jnp.concatenate(split(step(come_ref[...], t_ref, e_ref)), 0)
        near_ref[...] = near
        fill(far_ref, split(step(near, mt_ref, me_ref)))
        v_ref[...] = come_ref[...]


def double_kernel(core_ref, come_ref, e_ref, t_ref, me_ref, mt_ref, m1_ref, near_ref, far_ref):
    def body(x1, y1, x2, y2):
        near = jnp.concatenate(split(step(come_ref[...], x1, y1)), 0)
        near_ref[...] = near
        far_ref[...] = jnp.concatenate(split(step(near, x2, y2)), 0)

    by_role(core_ref, body, (e_ref, t_ref, me_ref, mt_ref))


def blocks(ref):
    return [ref[W * b : W * (b + 1), :] for b in range(ref.shape[0] // W)]


def fill(ref, parts):
    for b, part in enumerate(parts):
        ref[W * b : W * (b + 1), :] = part


def pairs_of(z_ref, x_ref, w_ref, put):
    n = z_ref.shape[0] // W
    for t in range(x_ref.shape[1] // (2 * W)):
        mid = dot(z_ref[...], x_ref[:, 2 * W * t : 2 * W * (t + 1)]).astype(BF)
        for half in range(2):
            flat = jnp.concatenate([mid[W * k : W * (k + 1), W * half : W * (half + 1)] for k in range(n)], 1)
            put(2 * t + half, dot(flat, w_ref[...]))


def place(core_ref, z_ref, w_ref, v, u):
    @pl.when(core_ref[0] == 0)
    def _():
        fill(z_ref, v)
        fill(w_ref, u)

    @pl.when(core_ref[0] != 0)
    def _():
        fill(z_ref, u)
        fill(w_ref, v)


def proj_early_kernel(core_ref, v_ref, r1_ref, m1_ref, m2_ref, edge_ref, out_ref, z_ref, w_ref):
    place(core_ref, z_ref, w_ref, [v_ref[W:, :]] + blocks(r1_ref), blocks(m2_ref)[::-1] + [m1_ref[W:, :]])

    def put(p, value):
        out_ref[:, W * p : W * (p + 1)] = value

    pairs_of(z_ref, edge_ref, w_ref, put)


def pass_kernel(value_ref, after_ref, out_ref):
    out_ref[...] = value_ref[...]


def proj_late_kernel(core_ref, r2_ref, m1_ref, last_ref, edge_ref, early_ref, out_ref, z_ref, w_ref):
    place(core_ref, z_ref, w_ref, blocks(r2_ref), [m1_ref[:W, :], last_ref[...]])

    def put(p, value):
        at = slice(W * p, W * (p + 1))
        out_ref[:, at] = early_ref[:, at] + value

    pairs_of(z_ref, edge_ref, w_ref, put)


def proj_last_kernel(
    core_ref, v_ref, m3_ref, e_ref, me_ref, mt_ref, sum_ref, near_out_ref, out_ref,
    near_ref, z_ref, w_ref, stage_ref, sem, near_sem,
):
    def body(x1, y1, x2, y2):
        near_ref[...] = step(m3_ref[:W, :], y2, x2)

    by_role(core_ref, body, (None, None, me_ref, mt_ref))
    copies = [pltpu.make_async_copy(near_ref, near_out_ref, near_sem.at[0])]
    copies[0].start()
    place(core_ref, z_ref, w_ref, [v_ref[:W, :]], [near_ref[...]])
    pieces = sem.shape[0]
    each = e_ref.shape[1] // W // pieces

    def put(p, value):
        at = slice(W * p, W * (p + 1))
        stage_ref[:, at] = (sum_ref[:, at] + value).astype(BF)
        if (p + 1) % each == 0:
            at = pl.ds(W * (p + 1 - each), W * each)
            copies.append(pltpu.make_async_copy(stage_ref.at[:, at], out_ref.at[:, at], sem.at[p // each]))
            copies[-1].start()

    pairs_of(z_ref, e_ref, w_ref, put)
    for copy in copies:
        copy.wait()


def edge_kernel(
    core_ref, v_ref, r1_ref, r2_ref, near_ref, m2_ref, m1_ref, last_ref, edge_ref, turned_ref,
    out_ref, grad_ref, z_ref, w_ref, sem,
):
    def halves(ref):
        return [ref.at[pl.ds(0, W)], ref.at[pl.ds(W, W)]]

    v = halves(v_ref) + halves(r1_ref) + halves(r2_ref)
    u = [near_ref] + halves(m2_ref)[::-1] + halves(m1_ref)[::-1] + [last_ref]

    def fetch(z_parts, w_parts):
        copies = []
        for n, part in enumerate(z_parts + w_parts):
            k = n % len(z_parts)
            to = z_ref if n < len(z_parts) else w_ref
            copies.append(pltpu.make_async_copy(part, to.at[pl.ds(W * k, W)], sem.at[n]))
        for copy in copies:
            copy.start()
        for copy in copies:
            copy.wait()

    @pl.when(core_ref[0] == 0)
    def _():
        fetch(u, v)

    @pl.when(core_ref[0] != 0)
    def _():
        fetch(v[::-1], u[::-1])

    def put(p, value):
        out_ref[:, W * p : W * (p + 1)] = value.T.astype(BF)

    pairs_of(z_ref, turned_ref, w_ref, put)
    grad_ref[...] = step(z_ref[:W, :], turned_ref, edge_ref).astype(F32).T.astype(BF)


def gather_kernel(parts_ref, out_ref, in_ref, sem):
    rows = parts_ref.shape[1]
    planes = parts_ref.shape[2] // W
    pieces = sem.shape[0]
    each = planes // pieces
    copies = []
    for n in range(pieces):
        at = pl.ds(n * each * W, each * W)
        copies.append(pltpu.make_async_copy(parts_ref.at[:, :, at], in_ref.at[:, :, at], sem.at[n]))
        copies[-1].start()
    for p in range(planes):
        if p % each == 0:
            copies[p // each].wait()
        out_ref[pl.ds(p, rows, stride=planes), :] = jnp.sum(in_ref[:, :, W * p : W * (p + 1)].astype(F32), axis=0)


def call(kernel, shapes, *args, scratch=(), sems=(), flops=0, far=(), free=(), far_outs=(), alias=None, room=16):
    def spec(n, arg):
        if n in far or n in free:
            return pl.BlockSpec(memory_space=pl.ANY)
        return pl.BlockSpec(memory_space=pltpu.SMEM if arg.dtype == jnp.int32 else pltpu.VMEM)

    moved = sum(arg.size * arg.dtype.itemsize for arg in args)
    single = len(shapes) == 1
    outs = [
        pltpu.HBM(shape, kind) if n in far_outs else jax.ShapeDtypeStruct(shape, kind)
        for n, (shape, kind) in enumerate(shapes)
    ]
    out_specs = [pl.BlockSpec(memory_space=pl.ANY if n in far_outs else pltpu.VMEM) for n in range(len(shapes))]
    in_specs = [spec(n, arg) for n, arg in enumerate(args)]
    args = [pltpu.with_memory_space_constraint(arg, pltpu.HBM) if n in far else arg for n, arg in enumerate(args)]
    return pl.pallas_call(
        kernel,
        out_shape=outs[0] if single else outs,
        in_specs=in_specs,
        out_specs=out_specs[0] if single else out_specs,
        scratch_shapes=[pltpu.VMEM(shape, kind) for shape, kind in scratch]
        + [pltpu.SemaphoreType.DMA((count,)) for count in sems],
        input_output_aliases=alias or {},
        compiler_params=pltpu.CompilerParams(vmem_limit_bytes=room * 1024 * 1024),
        cost_estimate=pl.CostEstimate(flops=flops, bytes_accessed=moved, transcendentals=0),
    )(*args)


def shards(corners, edges, projectors, cotangent):
    corner = corners[0, 0]
    edge = edges[0, 0]
    projector = projectors[0]
    cot = cotangent[0, 0]
    width = edge.shape[1]
    rows = lax.axis_size("row")
    cols = lax.axis_size("col")
    core = (lax.axis_index("col") % 2).astype(jnp.int32).reshape(1)
    unit = 2 * W * W * width

    def send(value, to):
        pairs = [(i, to(i) % cols) for i in range(cols) if to(i) is not None]
        return lax.ppermute(value, "col", pairs)

    def swap(value):
        return send(value, lambda i: i ^ 1)

    def onward(value):
        return send(value, lambda i: i + 2 if i % 2 == 0 else i - 2)

    one, two = ((W, W), BF), ((2 * W, W), BF)
    whole, wide = ((W, width), BF), ((W, width), F32)

    def stacks(n):
        return [((n * W, W), BF), ((n * W, W), BF)]

    mate_cot = swap(cot)
    far_edge = swap(edge)
    turned, edge, corner, cot_t = call(
        turn_kernel, [whole, whole, one, one], projector, edge, corner, cot,
        scratch=[((width, W), BF), ((width, W), F32), ((W, W), BF)], sems=(4, 3), flops=unit, far=(0, 1, 2, 3),
    )
    u0, first, turned = call(
        own_kernel, [one, two, whole], core, corner, cot_t, mate_cot, edge, turned, flops=2 * unit, alias={5: 2}
    )
    r0 = send(first, lambda i: i - 1 if i % 2 == 0 else i + 1)
    far_turned = swap(turned)
    keep, ahead, mate_edge, mate_turned = call(
        ahead_kernel, [one, one, whole, whole], core, corner, edge, turned, far_edge, far_turned,
        sems=(2,), flops=4 * unit, free=(4, 5),
    )
    tensors = (edge, turned, mate_edge, mate_turned)
    v, near1, go1 = call(first_kernel, [two, two, two], core, r0, corner, keep, ahead, *tensors, flops=4 * unit)
    r1 = onward(go1)
    m1 = swap(near1)
    near2, go2 = call(double_kernel, [two, two], core, r1, *tensors, m1, flops=8 * unit)
    r2 = onward(go2)
    m2 = swap(near2)
    early = call(proj_early_kernel, [wide], core, v, r1, m1, m2, edge, scratch=stacks(3), flops=6 * unit)
    r2 = call(pass_kernel, [two], r2, early, free=(1,))
    m3 = swap(r2)
    late = call(proj_late_kernel, [wide], core, r2, m1, u0, edge, early, scratch=stacks(2), flops=4 * unit, alias={5: 0})
    near3, done = call(
        proj_last_kernel, [one, whole], core, v, m3, edge, mate_edge, mate_turned, late,
        scratch=[one] + stacks(1) + [whole], sems=(18, 1), flops=4 * unit, far_outs=(0, 1),
    )
    share = W // rows
    parts = lax.all_to_all(done.reshape(rows, share, width), "row", 0, 0, tiled=True)
    edge_grad, corner_grad = call(
        edge_kernel, [whole, one], core, v, r1, r2, near3, m2, m1, u0, edge, turned,
        scratch=stacks(6), sems=(12,), flops=14 * unit, room=63, far=range(1, 8),
    )
    proj = call(
        gather_kernel, [((share * width // W, W), F32)], parts,
        scratch=[((rows, share, width), BF)], sems=(6,), flops=unit, far=(0,),
    )
    return (corner_grad[None, None], edge_grad[None, None], proj[None])


def solution(mesh):
    placed = (
        P("row", "col", None, None),
        P("row", "col", None, None),
        P("col", None, None),
        P("row", "col", None, None),
    )
    return jax.shard_map(
        shards,
        mesh=mesh,
        in_specs=placed,
        out_specs=(P("row", "col", None, None), P("row", "col", None, None), P("col", "row", None)),
        check_vma=False,
    )
```

```python
import jax
import jax.numpy as jnp
from jax import lax
from jax.experimental import pallas as pl
from jax.experimental.pallas import tpu as pltpu
from jax.sharding import PartitionSpec as P


W = 128
BF = jnp.bfloat16
F32 = jnp.float32


def dot(a, b):
    return jnp.dot(a, b, preferred_element_type=F32)


def step(z, x_ref, y_ref):
    n = z.shape[0] // W
    total = None
    for t in range(x_ref.shape[1] // (2 * W)):
        cols = slice(2 * W * t, 2 * W * (t + 1))
        mid = dot(z, x_ref[:, cols]).astype(BF)
        tall = jnp.concatenate(
            [jnp.concatenate([mid[W * b : W * (b + 1), :W], mid[W * b : W * (b + 1), W:]], 0) for b in range(n)], 1
        )
        part = dot(y_ref[:, cols], tall)
        total = part if total is None else total + part
    return total.astype(BF)


def split(wide):
    return [wide[:, W * b : W * (b + 1)] for b in range(wide.shape[1] // W)]


def turn_kernel(
    proj_ref, edge_in, corner_in, cot_ref, turned_ref, edge_ref, corner_ref, cot_t_ref,
    proj_vmem, wide_ref, cot_vmem, proj_sem, sem,
):
    pieces = proj_sem.shape[0]
    size = proj_ref.shape[0] // pieces
    loads = []
    for n in range(pieces):
        at = pl.ds(n * size, size)
        loads.append(pltpu.make_async_copy(proj_ref.at[at], proj_vmem.at[at], proj_sem.at[n]))
    others = [
        pltpu.make_async_copy(cot_ref, cot_vmem, sem.at[0]),
        pltpu.make_async_copy(corner_in, corner_ref, sem.at[1]),
        pltpu.make_async_copy(edge_in, edge_ref, sem.at[2]),
    ]
    for copy in loads + others:
        copy.start()
    for n, copy in enumerate(loads):
        copy.wait()
        at = slice(n * size, (n + 1) * size)
        wide_ref[at, :] = proj_vmem[at, :].astype(F32)
    planes = turned_ref.shape[1] // W
    for p in range(planes):
        turned_ref[:, W * p : W * (p + 1)] = wide_ref[pl.ds(p, W, stride=planes), :].T.astype(BF)
    for copy in others:
        copy.wait()
    cot_t_ref[...] = cot_vmem[...].astype(F32).T.astype(BF)


def own_kernel(core_ref, corner_ref, cot_t_ref, mate_cot_ref, edge_ref, turned_ref, last_ref, send_ref, same_ref):
    @pl.when(core_ref[0] == 0)
    def _():
        last = mate_cot_ref[...].astype(F32).T.astype(BF)
        last_ref[...] = last
        send_ref[:W, :] = cot_t_ref[...]
        send_ref[W:, :] = step(last, turned_ref, edge_ref)

    @pl.when(core_ref[0] != 0)
    def _():
        last_ref[...] = corner_ref[...]
        moved = step(corner_ref[...], edge_ref, turned_ref)
        send_ref[:W, :] = moved
        send_ref[W:, :] = moved


def by_role(core_ref, body, tensors):
    edge, turned, mate_edge, mate_turned = tensors

    @pl.when(core_ref[0] == 0)
    def _():
        body(edge, turned, mate_edge, mate_turned)

    @pl.when(core_ref[0] != 0)
    def _():
        body(turned, edge, mate_turned, mate_edge)


def ahead_kernel(
    core_ref, corner_ref, e_ref, t_ref, far_edge_ref, far_turned_ref, keep_ref, out_ref, me_ref, mt_ref, sem
):
    copies = [
        pltpu.make_async_copy(far_edge_ref, me_ref, sem.at[0]),
        pltpu.make_async_copy(far_turned_ref, mt_ref, sem.at[1]),
    ]
    for copy in copies:
        copy.start()

    @pl.when(core_ref[0] == 0)
    def _():
        keep_ref[...] = step(corner_ref[...], e_ref, t_ref)

    for copy in copies:
        copy.wait()

    @pl.when(core_ref[0] == 0)
    def _():
        out_ref[...] = step(keep_ref[...], me_ref, mt_ref)

    @pl.when(core_ref[0] != 0)
    def _():
        keep_ref[...] = jnp.zeros_like(keep_ref)
        out_ref[...] = jnp.zeros_like(out_ref)


def first_kernel(
    core_ref, come_ref, corner_ref, keep_ref, ahead_ref, e_ref, t_ref, me_ref, mt_ref, v_ref, near_ref, far_ref
):
    @pl.when(core_ref[0] == 0)
    def _():
        near = step(come_ref[:W, :], e_ref, t_ref)
        fill(near_ref, [keep_ref[...], near])
        fill(far_ref, [ahead_ref[...], step(near, me_ref, mt_ref)])
        fill(v_ref, [corner_ref[...], come_ref[:W, :]])

    @pl.when(core_ref[0] != 0)
    def _():
        near = jnp.concatenate(split(step(come_ref[...], t_ref, e_ref)), 0)
        near_ref[...] = near
        fill(far_ref, split(step(near, mt_ref, me_ref)))
        v_ref[...] = come_ref[...]


def double_kernel(core_ref, come_ref, e_ref, t_ref, me_ref, mt_ref, m1_ref, near_ref, far_ref):
    def body(x1, y1, x2, y2):
        near = jnp.concatenate(split(step(come_ref[...], x1, y1)), 0)
        near_ref[...] = near
        far_ref[...] = jnp.concatenate(split(step(near, x2, y2)), 0)

    by_role(core_ref, body, (e_ref, t_ref, me_ref, mt_ref))


def blocks(ref):
    return [ref[W * b : W * (b + 1), :] for b in range(ref.shape[0] // W)]


def fill(ref, parts):
    for b, part in enumerate(parts):
        ref[W * b : W * (b + 1), :] = part


def pairs_of(z_ref, x_ref, w_ref, put):
    n = z_ref.shape[0] // W
    for t in range(x_ref.shape[1] // (2 * W)):
        mid = dot(z_ref[...], x_ref[:, 2 * W * t : 2 * W * (t + 1)]).astype(BF)
        for half in range(2):
            flat = jnp.concatenate([mid[W * k : W * (k + 1), W * half : W * (half + 1)] for k in range(n)], 1)
            put(2 * t + half, dot(flat, w_ref[...]))


def place(core_ref, z_ref, w_ref, v, u):
    @pl.when(core_ref[0] == 0)
    def _():
        fill(z_ref, v)
        fill(w_ref, u)

    @pl.when(core_ref[0] != 0)
    def _():
        fill(z_ref, u)
        fill(w_ref, v)


def proj_early_kernel(core_ref, v_ref, r1_ref, m1_ref, m2_ref, edge_ref, out_ref, z_ref, w_ref):
    place(core_ref, z_ref, w_ref, [v_ref[W:, :]] + blocks(r1_ref), blocks(m2_ref)[::-1] + [m1_ref[W:, :]])

    def put(p, value):
        out_ref[:, W * p : W * (p + 1)] = value

    pairs_of(z_ref, edge_ref, w_ref, put)


def pass_kernel(value_ref, after_ref, out_ref):
    out_ref[...] = value_ref[...]


def proj_late_kernel(core_ref, r2_ref, m1_ref, last_ref, edge_ref, early_ref, out_ref, z_ref, w_ref):
    place(core_ref, z_ref, w_ref, blocks(r2_ref), [m1_ref[:W, :], last_ref[...]])

    def put(p, value):
        at = slice(W * p, W * (p + 1))
        out_ref[:, at] = early_ref[:, at] + value

    pairs_of(z_ref, edge_ref, w_ref, put)


def proj_last_kernel(
    core_ref, v_ref, m3_ref, e_ref, me_ref, mt_ref, sum_ref, near_out_ref, *rest
):
    *out_refs, near_ref, z_ref, w_ref, stage_ref, sem, near_sem = rest

    def body(x1, y1, x2, y2):
        near_ref[...] = step(m3_ref[:W, :], y2, x2)

    by_role(core_ref, body, (None, None, me_ref, mt_ref))
    copies = [pltpu.make_async_copy(near_ref, near_out_ref, near_sem.at[0])]
    copies[0].start()
    share = out_refs[0].shape[0]
    place(core_ref, z_ref, w_ref, [v_ref[:W, :]], [near_ref[...]])
    pieces = sem.shape[0]
    each = e_ref.shape[1] // W // pieces

    def put(p, value):
        at = slice(W * p, W * (p + 1))
        stage_ref[:, at] = (sum_ref[:, at] + value).astype(BF)
        if (p + 1) % each == 0:
            at = pl.ds(W * (p + 1 - each), W * each)
            for k, ref in enumerate(out_refs):
                mine = pl.multiple_of(share * (core_ref[1] ^ k), share)
                copies.append(
                    pltpu.make_async_copy(stage_ref.at[pl.ds(mine, share), at], ref.at[:, at], sem.at[p // each, k])
                )
                copies[-1].start()

    pairs_of(z_ref, e_ref, w_ref, put)
    for copy in copies:
        copy.wait()


def edge_kernel(
    core_ref, v_ref, r1_ref, r2_ref, near_ref, m2_ref, m1_ref, last_ref, edge_ref, turned_ref,
    out_ref, grad_ref, z_ref, w_ref, sem,
):
    def halves(ref):
        return [ref.at[pl.ds(0, W)], ref.at[pl.ds(W, W)]]

    v = halves(v_ref) + halves(r1_ref) + halves(r2_ref)
    u = [near_ref] + halves(m2_ref)[::-1] + halves(m1_ref)[::-1] + [last_ref]

    def fetch(z_parts, w_parts):
        copies = []
        for n, part in enumerate(z_parts + w_parts):
            k = n % len(z_parts)
            to = z_ref if n < len(z_parts) else w_ref
            copies.append(pltpu.make_async_copy(part, to.at[pl.ds(W * k, W)], sem.at[n]))
        for copy in copies:
            copy.start()
        for copy in copies:
            copy.wait()

    @pl.when(core_ref[0] == 0)
    def _():
        fetch(u, v)

    @pl.when(core_ref[0] != 0)
    def _():
        fetch(v[::-1], u[::-1])

    def put(p, value):
        out_ref[:, W * p : W * (p + 1)] = value.T.astype(BF)

    pairs_of(z_ref, turned_ref, w_ref, put)
    grad_ref[...] = step(z_ref[:W, :], turned_ref, edge_ref).astype(F32).T.astype(BF)


def gather_kernel(*refs):
    *parts, out_ref = refs
    rows = parts[0].shape[0]
    planes = parts[0].shape[1] // W
    for p in range(planes):
        total = sum(part[:, W * p : W * (p + 1)].astype(F32) for part in parts)
        out_ref[pl.ds(p, rows, stride=planes), :] = total


def call(kernel, shapes, *args, scratch=(), sems=(), flops=0, far=(), free=(), far_outs=(), alias=None):
    def spec(n, arg):
        if n in far or n in free:
            return pl.BlockSpec(memory_space=pl.ANY)
        return pl.BlockSpec(memory_space=pltpu.SMEM if arg.dtype == jnp.int32 else pltpu.VMEM)

    moved = sum(arg.size * arg.dtype.itemsize for arg in args)
    single = len(shapes) == 1
    outs = [
        pltpu.HBM(shape, kind) if n in far_outs else jax.ShapeDtypeStruct(shape, kind)
        for n, (shape, kind) in enumerate(shapes)
    ]
    out_specs = [pl.BlockSpec(memory_space=pl.ANY if n in far_outs else pltpu.VMEM) for n in range(len(shapes))]
    in_specs = [spec(n, arg) for n, arg in enumerate(args)]
    args = [pltpu.with_memory_space_constraint(arg, pltpu.HBM) if n in far else arg for n, arg in enumerate(args)]
    return pl.pallas_call(
        kernel,
        out_shape=outs[0] if single else outs,
        in_specs=in_specs,
        out_specs=out_specs[0] if single else out_specs,
        scratch_shapes=[pltpu.VMEM(shape, kind) for shape, kind in scratch]
        + [pltpu.SemaphoreType.DMA(count if isinstance(count, tuple) else (count,)) for count in sems],
        input_output_aliases=alias or {},
        compiler_params=pltpu.CompilerParams(vmem_limit_bytes=16 * 1024 * 1024),
        cost_estimate=pl.CostEstimate(flops=flops, bytes_accessed=moved, transcendentals=0),
    )(*args)


def shards(corners, edges, projectors, cotangent):
    corner = corners[0, 0]
    edge = edges[0, 0]
    projector = projectors[0]
    cot = cotangent[0, 0]
    width = edge.shape[1]
    rows = lax.axis_size("row")
    cols = lax.axis_size("col")
    core = jnp.stack([lax.axis_index("col") % 2, lax.axis_index("row")]).astype(jnp.int32)
    share = W // rows
    unit = 2 * W * W * width

    def send(value, to):
        pairs = [(i, to(i) % cols) for i in range(cols) if to(i) is not None]
        return lax.ppermute(value, "col", pairs)

    def swap(value):
        return send(value, lambda i: i ^ 1)

    def onward(value):
        return send(value, lambda i: i + 2 if i % 2 == 0 else i - 2)

    one, two = ((W, W), BF), ((2 * W, W), BF)
    whole, wide = ((W, width), BF), ((W, width), F32)

    def stacks(n):
        return [((n * W, W), BF), ((n * W, W), BF)]

    mate_cot = swap(cot)
    far_edge = swap(edge)
    turned, edge, corner, cot_t = call(
        turn_kernel, [whole, whole, one, one], projector, edge, corner, cot,
        scratch=[((width, W), BF), ((width, W), F32), ((W, W), BF)], sems=(4, 3), flops=unit, far=(0, 1, 2, 3),
    )
    u0, first, turned = call(
        own_kernel, [one, two, whole], core, corner, cot_t, mate_cot, edge, turned, flops=2 * unit, alias={5: 2}
    )
    r0 = send(first, lambda i: i - 1 if i % 2 == 0 else i + 1)
    far_turned = swap(turned)
    keep, ahead, mate_edge, mate_turned = call(
        ahead_kernel, [one, one, whole, whole], core, corner, edge, turned, far_edge, far_turned,
        sems=(2,), flops=4 * unit, free=(4, 5),
    )
    tensors = (edge, turned, mate_edge, mate_turned)
    v, near1, go1 = call(first_kernel, [two, two, two], core, r0, corner, keep, ahead, *tensors, flops=4 * unit)
    r1 = onward(go1)
    m1 = swap(near1)
    near2, go2 = call(double_kernel, [two, two], core, r1, *tensors, m1, flops=8 * unit)
    r2 = onward(go2)
    m2 = swap(near2)
    early = call(proj_early_kernel, [wide], core, v, r1, m1, m2, edge, scratch=stacks(3), flops=6 * unit)
    r2 = call(pass_kernel, [two], r2, early, free=(1,))
    m3 = swap(r2)
    late = call(proj_late_kernel, [wide], core, r2, m1, u0, edge, early, scratch=stacks(2), flops=4 * unit, alias={5: 0})
    near3, *done = call(
        proj_last_kernel, [one] + [((share, width), BF)] * rows, core, v, m3, edge, mate_edge, mate_turned, late,
        scratch=[one] + stacks(1) + [whole], sems=((6, rows), 1), flops=4 * unit, far_outs=range(rows + 1),
    )
    parts = done[:1] + [
        lax.ppermute(done[k], "row", [(i, i ^ k) for i in range(rows)]) for k in range(1, rows)
    ]
    edge_grad, corner_grad = call(
        edge_kernel, [whole, one], core, v, r1, r2, near3, m2, m1, u0, edge, turned,
        scratch=stacks(6), sems=(12,), flops=14 * unit, far=range(1, 8),
    )
    proj = call(gather_kernel, [((share * width // W, W), F32)], *parts, flops=unit)
    return (corner_grad[None, None], edge_grad[None, None], proj[None])


def solution(mesh):
    placed = (
        P("row", "col", None, None),
        P("row", "col", None, None),
        P("col", None, None),
        P("row", "col", None, None),
    )
    return jax.shard_map(
        shards,
        mesh=mesh,
        in_specs=placed,
        out_specs=(P("row", "col", None, None), P("row", "col", None, None), P("col", "row", None)),
        check_vma=False,
    )
```

```python
import jax
import jax.numpy as jnp
from jax import lax
from jax.experimental import pallas as pl
from jax.experimental.pallas import tpu as pltpu
from jax.sharding import PartitionSpec as P


W = 128
BF = jnp.bfloat16
F32 = jnp.float32


def dot(a, b):
    return jnp.dot(a, b, preferred_element_type=F32)


def step(z, x_ref, y_ref):
    n = z.shape[0] // W
    total = None
    for t in range(x_ref.shape[1] // (2 * W)):
        cols = slice(2 * W * t, 2 * W * (t + 1))
        mid = dot(z, x_ref[:, cols]).astype(BF)
        tall = jnp.concatenate(
            [jnp.concatenate([mid[W * b : W * (b + 1), :W], mid[W * b : W * (b + 1), W:]], 0) for b in range(n)], 1
        )
        part = dot(y_ref[:, cols], tall)
        total = part if total is None else total + part
    return total.astype(BF)


def split(wide):
    return [wide[:, W * b : W * (b + 1)] for b in range(wide.shape[1] // W)]


def turn_kernel(
    proj_ref, edge_in, corner_in, cot_ref, turned_ref, edge_ref, corner_ref, cot_t_ref,
    proj_vmem, wide_ref, cot_vmem, proj_sem, sem,
):
    pieces = proj_sem.shape[0]
    size = proj_ref.shape[0] // pieces
    loads = []
    for n in range(pieces):
        at = pl.ds(n * size, size)
        loads.append(pltpu.make_async_copy(proj_ref.at[at], proj_vmem.at[at], proj_sem.at[n]))
    others = [
        pltpu.make_async_copy(cot_ref, cot_vmem, sem.at[0]),
        pltpu.make_async_copy(corner_in, corner_ref, sem.at[1]),
        pltpu.make_async_copy(edge_in, edge_ref, sem.at[2]),
    ]
    for copy in loads + others:
        copy.start()
    for n, copy in enumerate(loads):
        copy.wait()
        at = slice(n * size, (n + 1) * size)
        wide_ref[at, :] = proj_vmem[at, :].astype(F32)
    planes = turned_ref.shape[1] // W
    for p in range(planes):
        turned_ref[:, W * p : W * (p + 1)] = wide_ref[pl.ds(p, W, stride=planes), :].T.astype(BF)
    for copy in others:
        copy.wait()
    cot_t_ref[...] = cot_vmem[...].astype(F32).T.astype(BF)


def own_kernel(
    core_ref, corner_ref, cot_t_ref, mate_cot_ref, edge_ref, turned_ref, last_ref, send_ref, same_ref, mate_ref, sem
):
    @pl.when(core_ref[0] == 0)
    def _():
        copy = pltpu.make_async_copy(mate_cot_ref, mate_ref, sem.at[0])
        copy.start()
        copy.wait()
        last = mate_ref[...].astype(F32).T.astype(BF)
        last_ref[...] = last
        send_ref[:W, :] = cot_t_ref[...]
        send_ref[W:, :] = step(last, turned_ref, edge_ref)

    @pl.when(core_ref[0] != 0)
    def _():
        last_ref[...] = corner_ref[...]
        moved = step(corner_ref[...], edge_ref, turned_ref)
        send_ref[:W, :] = moved
        send_ref[W:, :] = moved


def by_role(core_ref, body, tensors):
    edge, turned, mate_edge, mate_turned = tensors

    @pl.when(core_ref[0] == 0)
    def _():
        body(edge, turned, mate_edge, mate_turned)

    @pl.when(core_ref[0] != 0)
    def _():
        body(turned, edge, mate_turned, mate_edge)


def ahead_kernel(
    core_ref, corner_ref, e_ref, t_ref, far_edge_ref, far_turned_ref, keep_ref, out_ref, me_ref, mt_ref, sem
):
    copies = [
        pltpu.make_async_copy(far_edge_ref, me_ref, sem.at[0]),
        pltpu.make_async_copy(far_turned_ref, mt_ref, sem.at[1]),
    ]
    for copy in copies:
        copy.start()

    @pl.when(core_ref[0] == 0)
    def _():
        keep_ref[...] = step(corner_ref[...], e_ref, t_ref)

    for copy in copies:
        copy.wait()

    @pl.when(core_ref[0] == 0)
    def _():
        out_ref[...] = step(keep_ref[...], me_ref, mt_ref)

    @pl.when(core_ref[0] != 0)
    def _():
        keep_ref[...] = jnp.zeros_like(keep_ref)
        out_ref[...] = jnp.zeros_like(out_ref)


def first_kernel(
    core_ref, come_ref, corner_ref, keep_ref, ahead_ref, e_ref, t_ref, me_ref, mt_ref, v_ref, near_ref, far_ref
):
    @pl.when(core_ref[0] == 0)
    def _():
        near = step(come_ref[:W, :], e_ref, t_ref)
        fill(near_ref, [keep_ref[...], near])
        fill(far_ref, [ahead_ref[...], step(near, me_ref, mt_ref)])
        fill(v_ref, [corner_ref[...], come_ref[:W, :]])

    @pl.when(core_ref[0] != 0)
    def _():
        near = jnp.concatenate(split(step(come_ref[...], t_ref, e_ref)), 0)
        near_ref[...] = near
        fill(far_ref, split(step(near, mt_ref, me_ref)))
        v_ref[...] = come_ref[...]


def double_kernel(core_ref, come_ref, e_ref, t_ref, me_ref, mt_ref, m1_ref, near_ref, far_ref):
    def body(x1, y1, x2, y2):
        near = jnp.concatenate(split(step(come_ref[...], x1, y1)), 0)
        near_ref[...] = near
        far_ref[...] = jnp.concatenate(split(step(near, x2, y2)), 0)

    by_role(core_ref, body, (e_ref, t_ref, me_ref, mt_ref))


def blocks(ref):
    return [ref[W * b : W * (b + 1), :] for b in range(ref.shape[0] // W)]


def fill(ref, parts):
    for b, part in enumerate(parts):
        ref[W * b : W * (b + 1), :] = part


def pairs_of(z_ref, x_ref, w_ref, put):
    n = z_ref.shape[0] // W
    for t in range(x_ref.shape[1] // (2 * W)):
        mid = dot(z_ref[...], x_ref[:, 2 * W * t : 2 * W * (t + 1)]).astype(BF)
        for half in range(2):
            flat = jnp.concatenate([mid[W * k : W * (k + 1), W * half : W * (half + 1)] for k in range(n)], 1)
            put(2 * t + half, dot(flat, w_ref[...]))


def place(core_ref, z_ref, w_ref, v, u):
    @pl.when(core_ref[0] == 0)
    def _():
        fill(z_ref, v)
        fill(w_ref, u)

    @pl.when(core_ref[0] != 0)
    def _():
        fill(z_ref, u)
        fill(w_ref, v)


def proj_early_kernel(core_ref, v_ref, r1_ref, m1_ref, m2_ref, edge_ref, out_ref, z_ref, w_ref):
    place(core_ref, z_ref, w_ref, [v_ref[W:, :]] + blocks(r1_ref), blocks(m2_ref)[::-1] + [m1_ref[W:, :]])

    def put(p, value):
        out_ref[:, W * p : W * (p + 1)] = value

    pairs_of(z_ref, edge_ref, w_ref, put)


def pass_kernel(value_ref, after_ref, out_ref):
    out_ref[...] = value_ref[...]


def proj_late_kernel(core_ref, r2_ref, m1_ref, last_ref, edge_ref, early_ref, out_ref, z_ref, w_ref):
    place(core_ref, z_ref, w_ref, blocks(r2_ref), [m1_ref[:W, :], last_ref[...]])

    def put(p, value):
        at = slice(W * p, W * (p + 1))
        out_ref[:, at] = early_ref[:, at] + value

    pairs_of(z_ref, edge_ref, w_ref, put)


def proj_last_kernel(
    core_ref, v_ref, m3_ref, e_ref, me_ref, mt_ref, sum_ref, near_out_ref, out_ref,
    near_ref, z_ref, w_ref, stage_ref, sem, near_sem,
):
    def body(x1, y1, x2, y2):
        near_ref[...] = step(m3_ref[:W, :], y2, x2)

    by_role(core_ref, body, (None, None, me_ref, mt_ref))
    copies = [pltpu.make_async_copy(near_ref, near_out_ref, near_sem.at[0])]
    copies[0].start()
    place(core_ref, z_ref, w_ref, [v_ref[:W, :]], [near_ref[...]])
    pieces = sem.shape[0]
    each = e_ref.shape[1] // W // pieces

    def put(p, value):
        at = slice(W * p, W * (p + 1))
        stage_ref[:, at] = (sum_ref[:, at] + value).astype(BF)
        if (p + 1) % each == 0:
            at = pl.ds(W * (p + 1 - each), W * each)
            copies.append(pltpu.make_async_copy(stage_ref.at[:, at], out_ref.at[:, at], sem.at[p // each]))
            copies[-1].start()

    pairs_of(z_ref, e_ref, w_ref, put)
    for copy in copies:
        copy.wait()


def edge_kernel(
    core_ref, v_ref, r1_ref, r2_ref, near_ref, m2_ref, m1_ref, last_ref, edge_ref, turned_ref,
    out_ref, grad_ref, z_ref, w_ref, sem,
):
    def halves(ref):
        return [ref.at[pl.ds(0, W)], ref.at[pl.ds(W, W)]]

    v = halves(v_ref) + halves(r1_ref) + halves(r2_ref)
    u = [near_ref] + halves(m2_ref)[::-1] + halves(m1_ref)[::-1] + [last_ref]

    def fetch(z_parts, w_parts):
        copies = []
        for n, part in enumerate(z_parts + w_parts):
            k = n % len(z_parts)
            to = z_ref if n < len(z_parts) else w_ref
            copies.append(pltpu.make_async_copy(part, to.at[pl.ds(W * k, W)], sem.at[n]))
        for copy in copies:
            copy.start()
        for copy in copies:
            copy.wait()

    @pl.when(core_ref[0] == 0)
    def _():
        fetch(u, v)

    @pl.when(core_ref[0] != 0)
    def _():
        fetch(v[::-1], u[::-1])

    def put(p, value):
        out_ref[:, W * p : W * (p + 1)] = value.T.astype(BF)

    pairs_of(z_ref, turned_ref, w_ref, put)
    grad_ref[...] = step(z_ref[:W, :], turned_ref, edge_ref).astype(F32).T.astype(BF)


def gather_kernel(parts_ref, out_ref):
    rows = parts_ref.shape[1]
    planes = parts_ref.shape[2] // W
    for p in range(planes):
        out_ref[pl.ds(p, rows, stride=planes), :] = jnp.sum(
            parts_ref[:, :, W * p : W * (p + 1)].astype(F32), axis=0
        )


def call(kernel, shapes, *args, scratch=(), sems=(), flops=0, far=(), free=(), far_outs=(), alias=None):
    def spec(n, arg):
        if n in far or n in free:
            return pl.BlockSpec(memory_space=pl.ANY)
        return pl.BlockSpec(memory_space=pltpu.SMEM if arg.dtype == jnp.int32 else pltpu.VMEM)

    moved = sum(arg.size * arg.dtype.itemsize for arg in args)
    single = len(shapes) == 1
    outs = [
        pltpu.HBM(shape, kind) if n in far_outs else jax.ShapeDtypeStruct(shape, kind)
        for n, (shape, kind) in enumerate(shapes)
    ]
    out_specs = [pl.BlockSpec(memory_space=pl.ANY if n in far_outs else pltpu.VMEM) for n in range(len(shapes))]
    in_specs = [spec(n, arg) for n, arg in enumerate(args)]
    args = [pltpu.with_memory_space_constraint(arg, pltpu.HBM) if n in far else arg for n, arg in enumerate(args)]
    return pl.pallas_call(
        kernel,
        out_shape=outs[0] if single else outs,
        in_specs=in_specs,
        out_specs=out_specs[0] if single else out_specs,
        scratch_shapes=[pltpu.VMEM(shape, kind) for shape, kind in scratch]
        + [pltpu.SemaphoreType.DMA((count,)) for count in sems],
        input_output_aliases=alias or {},
        compiler_params=pltpu.CompilerParams(vmem_limit_bytes=16 * 1024 * 1024),
        cost_estimate=pl.CostEstimate(flops=flops, bytes_accessed=moved, transcendentals=0),
    )(*args)


def shards(corners, edges, projectors, cotangent):
    corner = corners[0, 0]
    edge = edges[0, 0]
    projector = projectors[0]
    cot = cotangent[0, 0]
    width = edge.shape[1]
    rows = lax.axis_size("row")
    cols = lax.axis_size("col")
    core = (lax.axis_index("col") % 2).astype(jnp.int32).reshape(1)
    unit = 2 * W * W * width

    def send(value, to):
        pairs = [(i, to(i) % cols) for i in range(cols) if to(i) is not None]
        return lax.ppermute(value, "col", pairs)

    def swap(value):
        return send(value, lambda i: i ^ 1)

    def onward(value):
        return send(value, lambda i: i + 2 if i % 2 == 0 else i - 2)

    one, two = ((W, W), BF), ((2 * W, W), BF)
    whole, wide = ((W, width), BF), ((W, width), F32)

    def stacks(n):
        return [((n * W, W), BF), ((n * W, W), BF)]

    mate_cot = swap(cot)
    far_edge = swap(edge)
    turned, edge, corner, cot_t = call(
        turn_kernel, [whole, whole, one, one], projector, edge, corner, cot,
        scratch=[((width, W), BF), ((width, W), F32), ((W, W), BF)], sems=(4, 3), flops=unit, far=(0, 1, 2, 3),
    )
    u0, first, turned = call(
        own_kernel, [one, two, whole], core, corner, cot_t, mate_cot, edge, turned,
        scratch=[one], sems=(1,), flops=2 * unit, free=(3,), alias={5: 2},
    )
    r0 = send(first, lambda i: i - 1 if i % 2 == 0 else i + 1)
    far_turned = swap(turned)
    keep, ahead, mate_edge, mate_turned = call(
        ahead_kernel, [one, one, whole, whole], core, corner, edge, turned, far_edge, far_turned,
        sems=(2,), flops=4 * unit, free=(4, 5),
    )
    tensors = (edge, turned, mate_edge, mate_turned)
    v, near1, go1 = call(first_kernel, [two, two, two], core, r0, corner, keep, ahead, *tensors, flops=4 * unit)
    r1 = onward(go1)
    m1 = swap(near1)
    near2, go2 = call(double_kernel, [two, two], core, r1, *tensors, m1, flops=8 * unit)
    r2 = onward(go2)
    m2 = swap(near2)
    early = call(proj_early_kernel, [wide], core, v, r1, m1, m2, edge, scratch=stacks(3), flops=6 * unit)
    r2 = call(pass_kernel, [two], r2, early, free=(1,))
    m3 = swap(r2)
    late = call(proj_late_kernel, [wide], core, r2, m1, u0, edge, early, scratch=stacks(2), flops=4 * unit, alias={5: 0})
    near3, done = call(
        proj_last_kernel, [one, whole], core, v, m3, edge, mate_edge, mate_turned, late,
        scratch=[one] + stacks(1) + [whole], sems=(18, 1), flops=4 * unit, far_outs=(0, 1),
    )
    share = W // rows
    parts = lax.all_to_all(done.reshape(rows, share, width), "row", 0, 0, tiled=True)
    edge_grad, corner_grad = call(
        edge_kernel, [whole, one], core, v, r1, r2, near3, m2, m1, u0, edge, turned,
        scratch=stacks(6), sems=(12,), flops=14 * unit, far=range(1, 8),
    )
    proj = call(gather_kernel, [((share * width // W, W), F32)], parts, flops=unit)
    return (corner_grad[None, None], edge_grad[None, None], proj[None])


def solution(mesh):
    placed = (
        P("row", "col", None, None),
        P("row", "col", None, None),
        P("col", None, None),
        P("row", "col", None, None),
    )
    return jax.shard_map(
        shards,
        mesh=mesh,
        in_specs=placed,
        out_specs=(P("row", "col", None, None), P("row", "col", None, None), P("col", "row", None)),
        check_vma=False,
    )
```
